32 devices in a mesh: gx: 2 (over y), gy: 4 (over x, core), gz: 4 (over z).
Axes of the slice: x: 2, y: 2, z: 4, core: 2. Of those that a mesh axis runs over, the one named last changes fastest.
Arguments:
- conc: float32 [32, 64, 512], P('gx', 'gy', 'gz'), may hold values from 0 to 1
- right_side: float32 [32, 64, 512], P('gx', 'gy', 'gz'), may hold values from -6144 to 6144
- order_field: bfloat16 [8, 32, 64, 512], P(None, 'gx', 'gy', 'gz'), may hold values from 0 to 1
- grain_ids: int32 [2, 4, 32, 8], P('gx', 'gy', 'gz'), may hold values from 0 to 255, as said below
Outputs:
- solution: float32 [32, 64, 512], P('gx', 'gy', 'gz')
- mobility: float32 [32, 64, 512], P('gx', 'gy', 'gz')
The draws below stay inside these ranges and needn't reach their ends.
Inputs may be any that keep to these rules, and one draw needn't show every extreme that they name: `grain_ids`: the 8 ids of one block are distinct; neighbouring blocks share some grains, usually in other slots.
All inputs are finite; a program needn't handle non-finite values.
Results may differ from the reference program's by a relative error of at most 0.0019.
Values may be sent and summed in bfloat16 or wider, within the bound.
A program may use at most 128 MiB of HBM per device.

```python
import jax
import jax.numpy as jnp

SLOTS = 8
BRICK = 16
SMOOTH = 2
COARSE_SWEEPS = 8
NX = 32
NY = 64
NZ = 512
NBX = 2
NBY = 4
NBZ = 32


def draw_grain_ids(key, part):
    slot = jnp.arange(SLOTS, dtype=jnp.int32)
    step_x = slot % 2
    step_y = slot // 2 % 2
    step_z = slot // 4 % 2
    brick_x = jnp.arange(NBX, dtype=jnp.int32)[:, None, None, None]
    brick_y = jnp.arange(NBY, dtype=jnp.int32)[None, :, None, None]
    brick_z = jnp.arange(NBZ, dtype=jnp.int32)[None, None, :, None]
    grain = (brick_x + step_x) % NBX * (NBY * NBZ) + (brick_y + step_y) % NBY * NBZ + (brick_z + step_z) % NBZ
    grain = jnp.broadcast_to(grain, (NBX, NBY, NBZ, SLOTS))
    scores = jax.random.randint(key, (NBX, NBY, NBZ, SLOTS), 0, 1 << 20) * SLOTS + slot
    order = jnp.argsort(scores, axis=-1)
    return jnp.take_along_axis(grain, order, axis=-1).astype(jnp.int32)


def shard_levels(own_key, shape, shards, low, high):
    gain = 1.0
    for dim, shards_of in shards:
        draws = jax.random.uniform(jax.random.fold_in(jax.random.fold_in(own_key, 6), dim), (shards_of,), jnp.float32, low / len(shards), high / len(shards))
        gain = gain * jnp.repeat(jnp.exp(draws), shape[dim] // shards_of).reshape((-1,) + (1,) * (len(shape) - 1 - dim))
    return gain


def noise(stream_key, dims, deviation, limit, cuts=(), kind=jnp.bfloat16):
    values = jax.random.normal(stream_key, dims, jnp.float32) * deviation
    if len(cuts) > 0:
        values = shard_levels(stream_key, dims, cuts, -0.22, 0.18) * values
    return jnp.clip(values, min=-limit, max=limit).astype(kind)


def setup_inputs(seed: int = 0) -> dict:
    seeds = jax.random.split(jax.random.key(seed), 5)
    return {
        "conc": jnp.clip(1.0 * jax.random.uniform(seeds[0], (NX, NY, NZ), jnp.float32) ** shard_levels(seeds[0], (NX, NY, NZ), ((0, 2), (1, 4), (2, 4)), -0.2, 0.2), 0.0, 1.0),
        "right_side": noise(seeds[1], (NX, NY, NZ), 1000.0, 6144.0, ((0, 2), (1, 4), (2, 4)), jnp.float32),
        "order_field": jnp.clip(1.0 * jax.random.uniform(seeds[2], (SLOTS, NX, NY, NZ), jnp.float32) ** shard_levels(seeds[2], (SLOTS, NX, NY, NZ), ((1, 2), (2, 4), (3, 4)), -0.2, 0.2), 0.0, 1.0).astype(jnp.bfloat16),
        "grain_ids": draw_grain_ids(jax.random.fold_in(seeds[4], 71), 0),
    }


OMEGA = 0.8
TAU_FINE = 256.0


def mobility_field(conc, order_field, grain_ids):
    blocks = (BRICK, BRICK, BRICK)
    summed = jnp.zeros(conc.shape, jnp.float32)
    for spatial in range(3):
        for direction in (1, -1):
            edge = blocks[spatial] - 1 if direction == 1 else 0
            source = 0 if direction == 1 else blocks[spatial] - 1
            extent = order_field.shape
            split = extent[:spatial + 1] + (extent[spatial + 1] // blocks[spatial], blocks[spatial]) + extent[spatial + 2:]
            facing = jnp.take(order_field.reshape(split), source, axis=spatial + 2).astype(jnp.float32)
            facing = jnp.roll(facing, -direction, axis=spatial + 1)
            beside_ids = jnp.roll(grain_ids, -direction, axis=spatial)
            for slot in range(SLOTS):
                matches = (grain_ids[..., slot:slot + 1] == beside_ids).astype(jnp.float32)
                remapped = jnp.zeros(facing.shape[1:], jnp.float32)
                for other in range(SLOTS):
                    weight = matches[..., other]
                    for across in range(3):
                        if across != spatial:
                            weight = jnp.repeat(weight, blocks[across], axis=across)
                    remapped = remapped + weight * facing[other]
                field = order_field[slot].astype(jnp.float32)
                shifted = jnp.roll(field, -direction, axis=spatial)
                cell_split = field.shape[:spatial] + (field.shape[spatial] // blocks[spatial], blocks[spatial]) + field.shape[spatial + 1:]
                marker = (jnp.arange(blocks[spatial]) == edge).reshape((blocks[spatial],) + (1,) * (2 - spatial))
                shifted = jnp.where(marker, jnp.expand_dims(remapped, spatial + 1), shifted.reshape(cell_split)).reshape(field.shape)
                summed = summed + (shifted - field) ** 2
    return 1.0 + 8.0 * (conc * (1.0 - conc)) ** 2 + summed


def face_coeffs(mobility):
    result = []
    for spatial in range(3):
        result.append(0.5 * (mobility + jnp.roll(mobility, -1, axis=spatial)))
        result.append(0.5 * (mobility + jnp.roll(mobility, 1, axis=spatial)))
    return tuple(result)


def apply_operator(values, coeffs, diag, step):
    summed = None
    for spatial in range(3):
        plus_cell = jnp.roll(values, -1, axis=spatial)
        minus_cell = jnp.roll(values, 1, axis=spatial)
        term = coeffs[2 * spatial] * plus_cell + coeffs[2 * spatial + 1] * minus_cell
        summed = term if summed is None else summed + term
    return diag * values - step * summed


def diagonal_of(coeffs, step):
    summed = coeffs[0]
    for coeff in coeffs[1:]:
        summed = summed + coeff
    return 1.0 + step * summed


def jacobi_sweep(values, source, coeffs, diag, step):
    if values is None:
        return OMEGA * source / diag
    return values + OMEGA * (source - apply_operator(values, coeffs, diag, step)) / diag


def restrict_field(field):
    extent = field.shape
    grouped = field.reshape(extent[0] // 2, 2, extent[1] // 2, 2, extent[2] // 2, 2)
    return jnp.mean(grouped, axis=(1, 3, 5))


def restrict_coeffs(coeffs):
    result = []
    for position, coeff in enumerate(coeffs):
        spatial = position // 2
        pick = 1 if position % 2 == 0 else 0
        extent = coeff.shape
        grouped = coeff.reshape(extent[0] // 2, 2, extent[1] // 2, 2, extent[2] // 2, 2)
        chosen = jnp.take(grouped, pick, axis=2 * spatial + 1)
        remaining = tuple(pair_axis if pair_axis < 2 * spatial + 1 else pair_axis - 1 for pair_axis in (1, 3, 5) if pair_axis != 2 * spatial + 1)
        result.append(jnp.mean(chosen, axis=remaining))
    return tuple(result)


def prolong_field(field):
    return jnp.repeat(jnp.repeat(jnp.repeat(field, 2, axis=0), 2, axis=1), 2, axis=2)


def reference(conc, right_side, order_field, grain_ids):
    mobility = mobility_field(conc, order_field, grain_ids)
    coeffs_fine = face_coeffs(mobility)
    step_fine = TAU_FINE
    diag_fine = diagonal_of(coeffs_fine, step_fine)
    solution = conc
    for sweep_index in range(SMOOTH):
        solution = jacobi_sweep(solution, right_side, coeffs_fine, diag_fine, step_fine)
    fine_residual = right_side - apply_operator(solution, coeffs_fine, diag_fine, step_fine)
    source_mid = restrict_field(fine_residual)
    coeffs_mid = restrict_coeffs(coeffs_fine)
    step_mid = TAU_FINE / 4.0
    diag_mid = diagonal_of(coeffs_mid, step_mid)
    error_mid = None
    for sweep_index in range(SMOOTH):
        error_mid = jacobi_sweep(error_mid, source_mid, coeffs_mid, diag_mid, step_mid)
    mid_residual = source_mid - apply_operator(error_mid, coeffs_mid, diag_mid, step_mid)
    source_low = restrict_field(mid_residual)
    coeffs_low = restrict_coeffs(coeffs_mid)
    step_low = TAU_FINE / 16.0
    diag_low = diagonal_of(coeffs_low, step_low)
    error_low = None
    for sweep_index in range(COARSE_SWEEPS):
        error_low = jacobi_sweep(error_low, source_low, coeffs_low, diag_low, step_low)
    error_mid = error_mid + prolong_field(error_low)
    for sweep_index in range(SMOOTH):
        error_mid = jacobi_sweep(error_mid, source_mid, coeffs_mid, diag_mid, step_mid)
    solution = solution + prolong_field(error_mid)
    for sweep_index in range(SMOOTH):
        solution = jacobi_sweep(solution, right_side, coeffs_fine, diag_fine, step_fine)
    return solution, mobility
```

```python
import functools

import jax
import jax.numpy as jnp
from jax import lax
from jax.experimental import pallas as pl
from jax.experimental.pallas import tpu as pltpu
from jax.sharding import PartitionSpec as P

SLOTS = 8
BRICK = 16
COARSE_SWEEPS = 8
OMEGA = 0.8
TAU_FINE = 256.0
AXES = ("gx", "gy", "gz")
MESH = pl.DeviceIdType.MESH
HIGHEST = lax.Precision.HIGHEST


def kernel(counts, conc_ref, rhs_ref, order_ref, ids_ref, sol_ref, mob_ref, send, recv, order_y, order_z, order_recv_x,
           order_recv_y, order_recv_z, ids_send, ids_recv, rows_ref, fine_k, coeff0, coeff1, coeff2, send_sem,
           recv_sem, order_send_sem, order_recv_sem, ids_send_sem, ids_recv_sem):
    planes, rows, lanes = conc_ref.shape
    me = tuple(lax.axis_index(axis) for axis in AXES)

    def beside(dim, sign):
        index = list(me)
        index[dim] = lax.rem(me[dim] + sign + counts[dim], counts[dim])
        return tuple(index)

    targets = [beside(dim, sign) for dim in range(3) for sign in (1, -1)]

    barrier = pltpu.get_barrier_semaphore()
    for target in targets:
        pl.semaphore_signal(barrier, inc=1, device_id=target, device_id_type=MESH)
    pl.semaphore_wait(barrier, 6)

    row = lax.broadcasted_iota(jnp.int32, (rows, lanes), 0)
    lane = lax.broadcasted_iota(jnp.int32, (rows, lanes), 1)
    zero = jnp.zeros((rows, lanes), jnp.float32)
    started = []

    def start(source, dest, source_sem, dest_sem, face):
        copy = pltpu.make_async_remote_copy(
            src_ref=source, dst_ref=dest, send_sem=source_sem, recv_sem=dest_sem, device_id=targets[face],
            device_id_type=MESH)
        copy.start()
        started.append(copy)
        return copy

    def spread_row(line):
        return jnp.broadcast_to(line, (rows, lanes))

    def spread_lane(column):
        return jnp.broadcast_to(column, (rows, lanes))

    def send_faces(turn, field):
        count = len(field)
        copies = []

        def go(face, extent):
            copies.append(start(
                send.at[turn, face, pl.ds(0, extent)], recv.at[turn, face, pl.ds(0, extent)],
                send_sem.at[turn, face], recv_sem.at[turn, face], face))

        send[turn, 0] = field[-1]
        go(0, rows)
        send[turn, 1] = field[0]
        go(1, rows)
        extent = max(count, 8)
        for face, at in ((2, rows - 1), (3, 0)):
            for i in range(extent):
                send[turn, face, i:i + 1, :] = field[i % count][at:at + 1, :]
            go(face, extent)
        for face, at in ((4, lanes - 1), (5, 0)):
            packed = zero
            for i in range(count):
                packed = jnp.where(lane == i, spread_lane(field[i][:, at:at + 1]), packed)
            send[turn, face] = packed
            go(face, rows)
        return copies

    def edge_rows(turn, i):
        return jnp.where(row < rows // 2, spread_row(recv[turn, 2, i:i + 1, :]), spread_row(recv[turn, 3, i:i + 1, :]))

    def edge_lanes(minus, plus, i):
        return jnp.where(lane < lanes // 2, spread_lane(minus[:, i:i + 1]), spread_lane(plus[:, i:i + 1]))

    def wait(copies):
        for copy in copies:
            copy.wait_recv()

    ids = ids_ref[0, 0].astype(jnp.float32)
    blocks = ids.shape[0]
    shape = (blocks, lanes)
    chosen = (lax.broadcasted_iota(jnp.int32, shape, 1) // BRICK == lax.broadcasted_iota(jnp.int32, shape, 0))
    chosen = chosen.astype(jnp.float32)
    ids_lane = lax.dot_general(ids, chosen, (((0,), (0,)), ((), ())), precision=HIGHEST,
                               preferred_element_type=jnp.float32)
    ids_slot = lax.dot_general(ids, chosen, (((1,), (0,)), ((), ())), precision=HIGHEST,
                               preferred_element_type=jnp.float32)
    ids_send[0] = ids_lane
    ids_send[1] = ids_slot
    ids_copies = [
        start(ids_send.at[face // 4], ids_recv.at[face], ids_send_sem.at[face], ids_recv_sem.at[face], face)
        for face in range(6)
    ]
    order_copies = [
        start(order_ref.at[:, planes - 1], order_recv_x.at[0], order_send_sem.at[0], order_recv_sem.at[0], 0),
        start(order_ref.at[:, 0], order_recv_x.at[1], order_send_sem.at[1], order_recv_sem.at[1], 1),
    ]

    def pack(i, carry):
        last, first = carry
        for s in range(SLOTS):
            plane = order_ref[s, i].astype(jnp.float32)
            rows_ref[0, s, pl.ds(i, 1), :] = plane[rows - 1:rows, :]
            rows_ref[1, s, pl.ds(i, 1), :] = plane[0:1, :]
            here = lane == s * BRICK + i
            last = jnp.where(here, spread_lane(plane[:, lanes - 1:lanes]), last)
            first = jnp.where(here, spread_lane(plane[:, 0:1]), first)
        return last, first

    last, first = lax.fori_loop(0, planes, pack, (zero, zero))
    for face in range(2):
        order_y[face] = rows_ref[face].astype(jnp.bfloat16)
        order_copies.append(start(order_y.at[face], order_recv_y.at[face], order_send_sem.at[2 + face],
                                  order_recv_sem.at[2 + face], 2 + face))
    for face, value in ((0, last), (1, first)):
        order_z[face] = value.astype(jnp.bfloat16)
        order_copies.append(start(order_z.at[face], order_recv_z.at[face], order_send_sem.at[4 + face],
                                  order_recv_sem.at[4 + face], 4 + face))
    conc = [conc_ref[i] for i in range(planes)]
    conc_copies = send_faces(0, conc)

    id_lane = lax.broadcasted_iota(jnp.int32, shape, 1)
    ids_next = jnp.where(id_lane == lanes - 1, -1.0, pltpu.roll(ids_lane, lanes - 1, 1))
    ids_before = jnp.where(id_lane == 0, -1.0, pltpu.roll(ids_lane, 1, 1))
    matched, alone = [], []
    for s in range(SLOTS):
        own = jnp.broadcast_to(ids_lane[s:s + 1, :], shape)
        hit = jnp.sum((own == ids_next).astype(jnp.float32), axis=0, keepdims=True)
        matched.append(hit)
        hit = jnp.sum((own == ids_before).astype(jnp.float32), axis=0, keepdims=True)
        alone.append(jnp.where(lax.broadcasted_iota(jnp.int32, (1, lanes), 1) == 0, 0.0, 1.0 - hit))

    def remap(own_ids, other_ids, others):
        result = []
        for s in range(SLOTS):
            value = zero
            for t in range(SLOTS):
                value = jnp.where(spread_row(own_ids[s:s + 1, :]) == spread_row(other_ids[t:t + 1, :]), others[t], value)
            result.append(value)
        return result

    def inside(i, carry):
        above = jnp.minimum(i + 1, planes - 1)
        below = jnp.maximum(i - 1, 0)
        own = [order_ref[s, i].astype(jnp.float32) for s in range(SLOTS)]
        rolled = [pltpu.roll(plane, lanes - 1, 1) for plane in own]
        mapped = remap(ids_lane, ids_next, rolled)
        c = conc_ref[i]
        reaction = c * (1.0 - c)
        total = 1.0 + 8.0 * (reaction * reaction)
        along_y, along_z, shared = zero, zero, zero
        for s in range(SLOTS):
            differ = order_ref[s, above].astype(jnp.float32) - own[s]
            total = total + differ * differ
            differ = order_ref[s, below].astype(jnp.float32) - own[s]
            total = total + differ * differ
            differ = pltpu.roll(own[s], rows - 1, 0) - own[s]
            along_y = along_y + differ * differ
            differ = mapped[s] - own[s]
            square = differ * differ
            along_z = along_z + square
            shared = shared + matched[s] * square
            total = total + alone[s] * (own[s] * own[s])
        along_y = jnp.where(row == rows - 1, 0.0, along_y)
        along_z = jnp.where(lane == lanes - 1, 0.0, along_z)
        total = total + along_y + pltpu.roll(along_y, 1, 0)
        total = total + along_z + pltpu.roll(shared, 1, 1)
        mob_ref[i] = total
        return carry

    lax.fori_loop(0, planes, inside, 0)

    wait(ids_copies)
    wait(order_copies)
    for face, at in ((1, planes - 1), (0, 0)):
        others = [order_recv_x[face, t].astype(jnp.float32) for t in range(SLOTS)]
        mapped = remap(ids_lane, ids_recv[face], others)
        total = mob_ref[at]
        for s in range(SLOTS):
            differ = mapped[s] - order_ref[s, at].astype(jnp.float32)
            total = total + differ * differ
        mob_ref[at] = total
    across = []
    for face in (0, 1):
        others = [order_recv_y[face, t].astype(jnp.float32) for t in range(SLOTS)]
        mapped = remap(ids_lane, ids_recv[2 + face], others)
        total = zero
        for s in range(SLOTS):
            differ = mapped[s] - rows_ref[1 - face, s]
            total = total + differ * differ
        across.append(total)
    ends = []
    for face, own, block in ((0, first, 0), (1, last, blocks - 1)):
        own_ids = spread_row(ids_slot[block:block + 1, :])
        other_block = blocks - 1 - block
        other_ids = spread_row(ids_recv[4 + face, other_block:other_block + 1, :])
        others = order_recv_z[face].astype(jnp.float32)
        value = zero
        for shift in range(0, lanes, BRICK):
            same = own_ids == (pltpu.roll(other_ids, shift, 1) if shift else other_ids)
            value = jnp.where(same, pltpu.roll(others, shift, 1) if shift else others, value)
        differ = value - own
        total = differ * differ
        for shift in (64, 32, 16):
            total = total + pltpu.roll(total, shift, 1)
        ends.append(total)
    mobility = []
    for i in range(planes):
        total = mob_ref[i]
        total = total + jnp.where(row == 0, spread_row(across[0][i:i + 1, :]), 0.0)
        total = total + jnp.where(row == rows - 1, spread_row(across[1][i:i + 1, :]), 0.0)
        at_edge = jnp.logical_or(lane == 0, lane == lanes - 1)
        total = total + jnp.where(at_edge, edge_lanes(ends[0], ends[1], i), 0.0)
        mob_ref[i] = total
        mobility.append(total)
    copies = send_faces(1, mobility)
    wait(copies)

    minus, plus = recv[1, 4], recv[1, 5]
    for i in range(planes):
        own = mobility[i]
        rims = edge_rows(1, i)
        tips = edge_lanes(minus, plus, i)
        fine_k[0, i] = 0.5 * (own + (mobility[i + 1] if i < planes - 1 else recv[1, 1]))
        fine_k[1, i] = 0.5 * (own + (mobility[i - 1] if i > 0 else recv[1, 0]))
        fine_k[2, i] = 0.5 * (own + jnp.where(row == rows - 1, rims, pltpu.roll(own, rows - 1, 0)))
        fine_k[3, i] = 0.5 * (own + jnp.where(row == 0, rims, pltpu.roll(own, 1, 0)))
        fine_k[4, i] = 0.5 * (own + jnp.where(lane == lanes - 1, tips, pltpu.roll(own, lanes - 1, 1)))
        fine_k[5, i] = 0.5 * (own + jnp.where(lane == 0, tips, pltpu.roll(own, 1, 1)))

    def build(store, faces, tau, width):
        for i in range(len(faces[0])):
            k = [face[i] for face in faces]
            diag = 1.0 + tau * (k[0] + k[1] + k[2] + k[3] + k[4] + k[5])
            weight = OMEGA / diag
            scale = tau * weight
            store[0, i] = scale * k[0]
            store[1, i] = scale * k[1]
            top, bottom = row >= rows - width, row < width
            right, left = lane >= lanes - width, lane < width
            a, b = scale * k[2], scale * k[3]
            store[2, i] = jnp.where(top, 0.0, a)
            store[3, i] = jnp.where(bottom, 0.0, b)
            store[4, i] = jnp.where(top, a, jnp.where(bottom, b, 0.0))
            a, b = scale * k[4], scale * k[5]
            store[5, i] = jnp.where(right, 0.0, a)
            store[6, i] = jnp.where(left, 0.0, b)
            store[7, i] = jnp.where(right, a, jnp.where(left, b, 0.0))
            store[8, i] = weight
            store[9, i] = diag * (1.0 / OMEGA)

    def swap(value, dim, width):
        size = value.shape[dim]
        index = row if dim == 0 else lane
        upper = (index // width) % 2 == 1
        return upper, pltpu.roll(value, width, dim), pltpu.roll(value, size - width, dim)

    def mean_pair(value, dim, width):
        upper, down, up = swap(value, dim, width)
        return 0.5 * (value + jnp.where(upper, down, up))

    def take_upper(value, dim, width):
        upper, _, up = swap(value, dim, width)
        return jnp.where(upper, value, up)

    def take_lower(value, dim, width):
        upper, down, _ = swap(value, dim, width)
        return jnp.where(upper, down, value)

    def coarsen(faces, width):
        result = [[] for _ in range(6)]
        for i in range(len(faces[0]) // 2):
            def both(face):
                return 0.5 * (faces[face][2 * i] + faces[face][2 * i + 1])
            result[0].append(mean_pair(mean_pair(faces[0][2 * i + 1], 0, width), 1, width))
            result[1].append(mean_pair(mean_pair(faces[1][2 * i], 0, width), 1, width))
            result[2].append(mean_pair(take_upper(both(2), 0, width), 1, width))
            result[3].append(mean_pair(take_lower(both(3), 0, width), 1, width))
            result[4].append(mean_pair(take_upper(both(4), 1, width), 0, width))
            result[5].append(mean_pair(take_lower(both(5), 1, width), 0, width))
        return result

    def restrict(field, width):
        return [
            mean_pair(mean_pair(0.5 * (field[2 * i] + field[2 * i + 1]), 0, width), 1, width)
            for i in range(len(field) // 2)
        ]

    def sweep(turn, field, weighted, store, width, copies, keep, between=None):
        count = len(field)
        totals = []
        for i in range(count):
            own = field[i]
            total = keep * own + weighted[i]
            if i < count - 1:
                total = total + store[0, i] * field[i + 1]
            if i > 0:
                total = total + store[1, i] * field[i - 1]
            total = total + store[2, i] * pltpu.roll(own, rows - width, 0)
            total = total + store[3, i] * pltpu.roll(own, width, 0)
            total = total + store[5, i] * pltpu.roll(own, lanes - width, 1)
            total = total + store[6, i] * pltpu.roll(own, width, 1)
            totals.append(total)
        if between is not None:
            between()
        wait(copies)
        minus, plus = recv[turn, 4], recv[turn, 5]
        for i in range(count):
            total = totals[i] + store[4, i] * edge_rows(turn, i) + store[7, i] * edge_lanes(minus, plus, i)
            if i == count - 1:
                total = total + store[0, i] * recv[turn, 1]
            if i == 0:
                total = total + store[1, i] * recv[turn, 0]
            totals[i] = total
        return totals

    faces0 = [[fine_k[face, i] for i in range(planes)] for face in range(6)]
    build(coeff0, faces0, TAU_FINE, 1)
    weighted0 = [coeff0[8, i] * rhs_ref[i] for i in range(planes)]
    keep = 1.0 - OMEGA
    field = sweep(0, conc, weighted0, coeff0, 1, conc_copies, keep)

    faces1 = []

    def build_middle():
        faces1.extend(coarsen(faces0, 1))
        build(coeff1, faces1, TAU_FINE / 4.0, 2)

    copies = send_faces(2, field)
    field = sweep(2, field, weighted0, coeff0, 1, copies, keep, build_middle)

    def build_low():
        build(coeff2, coarsen(faces1, 2), TAU_FINE / 16.0, 4)

    copies = send_faces(3, field)
    added = sweep(3, field, weighted0, coeff0, 1, copies, -OMEGA, build_low)
    source1 = restrict([added[i] * coeff0[9, i] for i in range(planes)], 1)
    middle = planes // 2
    weighted1 = [coeff1[8, i] * source1[i] for i in range(middle)]
    error1 = weighted1
    copies = send_faces(4, error1)
    error1 = sweep(4, error1, weighted1, coeff1, 2, copies, keep)
    copies = send_faces(5, error1)
    added = sweep(5, error1, weighted1, coeff1, 2, copies, -OMEGA)
    source2 = restrict([added[i] * coeff1[9, i] for i in range(middle)], 2)
    low = planes // 4
    weighted2 = [coeff2[8, i] * source2[i] for i in range(low)]
    error2 = weighted2
    turn = 6
    for _ in range(COARSE_SWEEPS - 1):
        copies = send_faces(turn, error2)
        error2 = sweep(turn, error2, weighted2, coeff2, 4, copies, keep)
        turn += 1
    error1 = [error1[i] + error2[i // 2] for i in range(middle)]
    for _ in range(2):
        copies = send_faces(turn, error1)
        error1 = sweep(turn, error1, weighted1, coeff1, 2, copies, keep)
        turn += 1
    field = [field[i] + error1[i // 2] for i in range(planes)]
    for _ in range(2):
        copies = send_faces(turn, field)
        field = sweep(turn, field, weighted0, coeff0, 1, copies, keep)
        turn += 1
    for i in range(planes):
        sol_ref[i] = field[i]
    for copy in started:
        copy.wait_send()


TURNS = 6 + (COARSE_SWEEPS - 1) + 4


def body(counts, conc, right_side, order_field, grain_ids):
    planes, rows, lanes = conc.shape
    blocks = grain_ids.shape[2]
    vmem = pl.BlockSpec(memory_space=pltpu.VMEM)
    f32, bf16 = jnp.float32, jnp.bfloat16
    dma = pltpu.SemaphoreType.DMA
    out = jax.ShapeDtypeStruct(conc.shape, f32)
    return pl.pallas_call(
        functools.partial(kernel, counts),
        out_shape=(out, out),
        in_specs=[vmem] * 4,
        out_specs=(vmem, vmem),
        scratch_shapes=[
            pltpu.VMEM((TURNS, 6, rows, lanes), f32),
            pltpu.VMEM((TURNS, 6, rows, lanes), f32),
            pltpu.VMEM((2, SLOTS, planes, lanes), bf16),
            pltpu.VMEM((2, rows, lanes), bf16),
            pltpu.VMEM((2, SLOTS, rows, lanes), bf16),
            pltpu.VMEM((2, SLOTS, planes, lanes), bf16),
            pltpu.VMEM((2, rows, lanes), bf16),
            pltpu.VMEM((2, blocks, lanes), f32),
            pltpu.VMEM((6, blocks, lanes), f32),
            pltpu.VMEM((2, SLOTS, planes, lanes), f32),
            pltpu.VMEM((6, planes, rows, lanes), f32),
            pltpu.VMEM((10, planes, rows, lanes), f32),
            pltpu.VMEM((10, planes // 2, rows, lanes), f32),
            pltpu.VMEM((10, planes // 4, rows, lanes), f32),
            dma((TURNS, 6)),
            dma((TURNS, 6)),
            dma((6,)),
            dma((6,)),
            dma((6,)),
            dma((6,)),
        ],
        compiler_params=pltpu.CompilerParams(
            collective_id=0, has_side_effects=True, vmem_limit_bytes=40 * 1024 * 1024
        ),
    )(conc, right_side, order_field, grain_ids)


def solution(mesh):
    counts = tuple(mesh.shape[axis] for axis in AXES)
    return jax.shard_map(
        functools.partial(body, counts),
        mesh=mesh,
        in_specs=(
            P("gx", "gy", "gz"),
            P("gx", "gy", "gz"),
            P(None, "gx", "gy", "gz"),
            P("gx", "gy", "gz", None),
        ),
        out_specs=(P("gx", "gy", "gz"), P("gx", "gy", "gz")),
        check_vma=False,
    )
```

```python
import functools

import jax
import jax.numpy as jnp
from jax import lax
from jax.experimental import pallas as pl
from jax.experimental.pallas import tpu as pltpu
from jax.sharding import PartitionSpec as P

SLOTS = 8
BRICK = 16
COARSE_SWEEPS = 8
OMEGA = 0.8
TAU_FINE = 256.0
AXES = ("gx", "gy", "gz")
MESH = pl.DeviceIdType.MESH
HIGHEST = lax.Precision.HIGHEST


def kernel(counts, conc_in, rhs_in, order_in, ids_in, sol_ref, mob_ref, conc_ref, rhs_ref, order_ref, ids_ref, rhs_wide,
           deep_send, deep_recv, send, recv, order_y, order_z, order_recv_x,
           order_recv_y, order_recv_z, ids_send, ids_recv, rows_ref, fine_k, coeff0, coeff1, coeff2, send_sem,
           recv_sem, order_send_sem, order_recv_sem, ids_send_sem, ids_recv_sem, deep_send_sem, deep_recv_sem, load_sem):
    planes, rows, lanes = conc_ref.shape
    wide = 2 * lanes
    half = lanes // 2
    loads = [
        pltpu.make_async_copy(source, dest, load_sem.at[position])
        for position, (source, dest) in enumerate(
            ((ids_in, ids_ref), (order_in, order_ref), (conc_in, conc_ref), (rhs_in, rhs_ref)))
    ]
    for load in loads:
        load.start()
    me = tuple(lax.axis_index(axis) for axis in AXES)

    def beside(dim, sign):
        index = list(me)
        index[dim] = lax.rem(me[dim] + sign + counts[dim], counts[dim])
        return tuple(index)

    targets = [beside(dim, sign) for dim in range(3) for sign in (1, -1)]

    barrier = pltpu.get_barrier_semaphore()
    for target in targets:
        pl.semaphore_signal(barrier, inc=1, device_id=target, device_id_type=MESH)
    pl.semaphore_wait(barrier, 6)
    for load in loads:
        load.wait()

    row = lax.broadcasted_iota(jnp.int32, (rows, lanes), 0)
    lane = lax.broadcasted_iota(jnp.int32, (rows, lanes), 1)
    zero = jnp.zeros((rows, lanes), jnp.float32)
    started = []

    def start(source, dest, source_sem, dest_sem, face):
        copy = pltpu.make_async_remote_copy(
            src_ref=source, dst_ref=dest, send_sem=source_sem, recv_sem=dest_sem, device_id=targets[face],
            device_id_type=MESH)
        copy.start()
        started.append(copy)
        return copy

    def spread_row(line):
        return jnp.broadcast_to(line, (rows, lanes))

    def spread_lane(column):
        return jnp.broadcast_to(column, (rows, lanes))

    wide_row = lax.broadcasted_iota(jnp.int32, (rows, wide), 0)
    wide_lane = lax.broadcasted_iota(jnp.int32, (rows, wide), 1)

    def fold(face, width):
        if width == 1:
            return face
        parity = lax.broadcasted_iota(jnp.int32, (face.shape[0], lanes), 1) % 2
        return jnp.where(parity == 0, face[:, :lanes], face[:, lanes:])

    def unfold(face, width):
        if width == 1:
            return face
        parity = lax.broadcasted_iota(jnp.int32, face.shape, 1) % 2
        own = jnp.where(parity == 0, face, pltpu.roll(face, 1, 1))
        other = jnp.where(parity == 0, pltpu.roll(face, lanes - 1, 1), face)
        return jnp.concatenate([own, other], axis=1)

    def send_faces(turn, field, width):
        count = len(field)
        extent = max(count, 8)
        span = pl.ds(0, wide if width == 1 else lanes)
        copies = []

        def go(face, extent):
            part = (turn, face, pl.ds(0, extent), span)
            copies.append(start(send.at[part], recv.at[part], send_sem.at[turn, face], recv_sem.at[turn, face], face))

        send[turn, 0, :, span] = fold(field[-1], width)
        go(0, rows)
        send[turn, 1, :, span] = fold(field[0], width)
        go(1, rows)
        for face, at in ((2, rows - 1), (3, 0)):
            for i in range(extent):
                send[turn, face, i:i + 1, span] = fold(field[i % count][at:at + 1, :], width)
            go(face, extent)
        return copies

    def get_faces(turn, count, width):
        extent = max(count, 8)
        span = pl.ds(0, wide if width == 1 else lanes)
        return [unfold(recv[turn, face, pl.ds(0, rows if face < 2 else extent), span], width) for face in range(4)]

    def edge_rows(faces, i):
        return jnp.where(wide_row < rows // 2, jnp.broadcast_to(faces[2][i:i + 1, :], (rows, wide)),
                         jnp.broadcast_to(faces[3][i:i + 1, :], (rows, wide)))

    def send_halves(kind, firsts, seconds):
        copies = []
        for face in range(2):
            for i in range(len(firsts)):
                if face == 0:
                    value = jnp.where(lane < half, pltpu.roll(firsts[i], half, 1), seconds[i])
                else:
                    value = jnp.where(lane < half, firsts[i], pltpu.roll(seconds[i], half, 1))
                deep_send[kind, face, i] = value
            part = (kind, face, pl.ds(0, len(firsts)))
            copies.append(start(deep_send.at[part], deep_recv.at[part], deep_send_sem.at[kind, face],
                                deep_recv_sem.at[kind, face], 4 + face))
        return copies

    def widen(kind, firsts, seconds):
        results = [], []
        for i in range(len(firsts)):
            below, above = deep_recv[kind, 0, i], deep_recv[kind, 1, i]
            other = jnp.where(lane < half, above, pltpu.roll(below, half, 1))
            results[0].append(jnp.concatenate([firsts[i], other], axis=1))
            other = jnp.where(lane < half, pltpu.roll(above, half, 1), below)
            results[1].append(jnp.concatenate([seconds[i], other], axis=1))
        return results

    def edge_lanes(minus, plus, i):
        return jnp.where(lane < lanes // 2, spread_lane(minus[:, i:i + 1]), spread_lane(plus[:, i:i + 1]))

    def wait(copies):
        for copy in copies:
            copy.wait_recv()

    ids = ids_ref[0, 0].astype(jnp.float32)
    blocks = ids.shape[0]
    shape = (blocks, lanes)
    chosen = (lax.broadcasted_iota(jnp.int32, shape, 1) // BRICK == lax.broadcasted_iota(jnp.int32, shape, 0))
    chosen = chosen.astype(jnp.float32)
    ids_lane = lax.dot_general(ids, chosen, (((0,), (0,)), ((), ())), precision=HIGHEST,
                               preferred_element_type=jnp.float32)
    ids_slot = lax.dot_general(ids, chosen, (((1,), (0,)), ((), ())), precision=HIGHEST,
                               preferred_element_type=jnp.float32)
    ids_send[0] = ids_lane
    ids_send[1] = ids_slot
    ids_copies = [
        start(ids_send.at[face // 4], ids_recv.at[face], ids_send_sem.at[face], ids_recv_sem.at[face], face)
        for face in range(6)
    ]
    order_copies = [
        start(order_ref.at[:, planes - 1], order_recv_x.at[0], order_send_sem.at[0], order_recv_sem.at[0], 0),
        start(order_ref.at[:, 0], order_recv_x.at[1], order_send_sem.at[1], order_recv_sem.at[1], 1),
    ]

    def pack(i, carry):
        last, first = carry
        for s in range(SLOTS):
            plane = order_ref[s, i].astype(jnp.float32)
            rows_ref[0, s, pl.ds(i, 1), :] = plane[rows - 1:rows, :]
            rows_ref[1, s, pl.ds(i, 1), :] = plane[0:1, :]
            here = lane == s * BRICK + i
            last = jnp.where(here, spread_lane(plane[:, lanes - 1:lanes]), last)
            first = jnp.where(here, spread_lane(plane[:, 0:1]), first)
        return last, first

    last, first = lax.fori_loop(0, planes, pack, (zero, zero))
    for face in range(2):
        order_y[face] = rows_ref[face].astype(jnp.bfloat16)
        order_copies.append(start(order_y.at[face], order_recv_y.at[face], order_send_sem.at[2 + face],
                                  order_recv_sem.at[2 + face], 2 + face))
    for face, value in ((0, last), (1, first)):
        order_z[face] = value.astype(jnp.bfloat16)
        order_copies.append(start(order_z.at[face], order_recv_z.at[face], order_send_sem.at[4 + face],
                                  order_recv_sem.at[4 + face], 4 + face))
    own_conc = [conc_ref[i] for i in range(planes)]
    own_rhs = [rhs_ref[i] for i in range(planes)]
    conc_copies = send_halves(0, own_conc, own_rhs)

    id_lane = lax.broadcasted_iota(jnp.int32, shape, 1)
    ids_next = jnp.where(id_lane == lanes - 1, -1.0, pltpu.roll(ids_lane, lanes - 1, 1))
    ids_before = jnp.where(id_lane == 0, -1.0, pltpu.roll(ids_lane, 1, 1))
    matched, alone = [], []
    for s in range(SLOTS):
        own = jnp.broadcast_to(ids_lane[s:s + 1, :], shape)
        hit = jnp.sum((own == ids_next).astype(jnp.float32), axis=0, keepdims=True)
        matched.append(hit)
        hit = jnp.sum((own == ids_before).astype(jnp.float32), axis=0, keepdims=True)
        alone.append(jnp.where(lax.broadcasted_iota(jnp.int32, (1, lanes), 1) == 0, 0.0, 1.0 - hit))

    def remap(own_ids, other_ids, others):
        result = []
        for s in range(SLOTS):
            value = zero
            for t in range(SLOTS):
                value = jnp.where(spread_row(own_ids[s:s + 1, :]) == spread_row(other_ids[t:t + 1, :]), others[t], value)
            result.append(value)
        return result

    def inside(i, carry):
        above = jnp.minimum(i + 1, planes - 1)
        below = jnp.maximum(i - 1, 0)
        own = [order_ref[s, i].astype(jnp.float32) for s in range(SLOTS)]
        rolled = [pltpu.roll(plane, lanes - 1, 1) for plane in own]
        mapped = remap(ids_lane, ids_next, rolled)
        c = conc_ref[i]
        reaction = c * (1.0 - c)
        total = 1.0 + 8.0 * (reaction * reaction)
        along_y, along_z, shared = zero, zero, zero
        for s in range(SLOTS):
            differ = order_ref[s, above].astype(jnp.float32) - own[s]
            total = total + differ * differ
            differ = order_ref[s, below].astype(jnp.float32) - own[s]
            total = total + differ * differ
            differ = pltpu.roll(own[s], rows - 1, 0) - own[s]
            along_y = along_y + differ * differ
            differ = mapped[s] - own[s]
            square = differ * differ
            along_z = along_z + square
            shared = shared + matched[s] * square
            total = total + alone[s] * (own[s] * own[s])
        along_y = jnp.where(row == rows - 1, 0.0, along_y)
        along_z = jnp.where(lane == lanes - 1, 0.0, along_z)
        total = total + along_y + pltpu.roll(along_y, 1, 0)
        total = total + along_z + pltpu.roll(shared, 1, 1)
        mob_ref[i] = total
        return carry

    lax.fori_loop(0, planes, inside, 0)

    wait(ids_copies)
    wait(order_copies)
    for face, at in ((1, planes - 1), (0, 0)):
        others = [order_recv_x[face, t].astype(jnp.float32) for t in range(SLOTS)]
        mapped = remap(ids_lane, ids_recv[face], others)
        total = mob_ref[at]
        for s in range(SLOTS):
            differ = mapped[s] - order_ref[s, at].astype(jnp.float32)
            total = total + differ * differ
        mob_ref[at] = total
    across = []
    for face in (0, 1):
        others = [order_recv_y[face, t].astype(jnp.float32) for t in range(SLOTS)]
        mapped = remap(ids_lane, ids_recv[2 + face], others)
        total = zero
        for s in range(SLOTS):
            differ = mapped[s] - rows_ref[1 - face, s]
            total = total + differ * differ
        across.append(total)
    ends = []
    for face, own, block in ((0, first, 0), (1, last, blocks - 1)):
        own_ids = spread_row(ids_slot[block:block + 1, :])
        other_block = blocks - 1 - block
        other_ids = spread_row(ids_recv[4 + face, other_block:other_block + 1, :])
        others = order_recv_z[face].astype(jnp.float32)
        value = zero
        for shift in range(0, lanes, BRICK):
            same = own_ids == (pltpu.roll(other_ids, shift, 1) if shift else other_ids)
            value = jnp.where(same, pltpu.roll(others, shift, 1) if shift else others, value)
        differ = value - own
        total = differ * differ
        for shift in (64, 32, 16):
            total = total + pltpu.roll(total, shift, 1)
        ends.append(total)
    mobility = []
    for i in range(planes):
        total = mob_ref[i]
        total = total + jnp.where(row == 0, spread_row(across[0][i:i + 1, :]), 0.0)
        total = total + jnp.where(row == rows - 1, spread_row(across[1][i:i + 1, :]), 0.0)
        at_edge = jnp.logical_or(lane == 0, lane == lanes - 1)
        total = total + jnp.where(at_edge, edge_lanes(ends[0], ends[1], i), 0.0)
        mob_ref[i] = total
        mobility.append(total)
    middle = planes // 2
    copies = send_halves(1, mobility[:middle], mobility[middle:])
    wait(conc_copies)
    conc, rhs = widen(0, own_conc, own_rhs)
    for i in range(planes):
        rhs_wide[i] = rhs[i]
    conc_copies = send_faces(0, conc, 1)
    wait(copies)
    lower, upper = widen(1, mobility[:middle], mobility[middle:])
    mobility = lower + upper
    copies = send_faces(1, mobility, 1)
    for i in range(planes):
        own = mobility[i]
        fine_k[4, i] = 0.5 * (own + pltpu.roll(own, wide - 1, 1))
        fine_k[5, i] = 0.5 * (own + pltpu.roll(own, 1, 1))
    wait(copies)
    faces = get_faces(1, planes, 1)
    for i in range(planes):
        own = mobility[i]
        rims = edge_rows(faces, i)
        fine_k[0, i] = 0.5 * (own + (mobility[i + 1] if i < planes - 1 else faces[1]))
        fine_k[1, i] = 0.5 * (own + (mobility[i - 1] if i > 0 else faces[0]))
        fine_k[2, i] = 0.5 * (own + jnp.where(wide_row == rows - 1, rims, pltpu.roll(own, rows - 1, 0)))
        fine_k[3, i] = 0.5 * (own + jnp.where(wide_row == 0, rims, pltpu.roll(own, 1, 0)))

    def build(store, faces, tau, width):
        for i in range(len(faces[0])):
            k = [face[i] for face in faces]
            diag = 1.0 + tau * (k[0] + k[1] + k[2] + k[3] + k[4] + k[5])
            weight = OMEGA / diag
            scale = tau * weight
            store[0, i] = scale * k[0]
            store[1, i] = scale * k[1]
            top, bottom = wide_row >= rows - width, wide_row < width
            a, b = scale * k[2], scale * k[3]
            store[2, i] = jnp.where(top, 0.0, a)
            store[3, i] = jnp.where(bottom, 0.0, b)
            store[4, i] = jnp.where(top, a, jnp.where(bottom, b, 0.0))
            store[5, i] = scale * k[4]
            store[6, i] = scale * k[5]
            store[7, i] = weight
            store[8, i] = diag * (1.0 / OMEGA)

    def swap(value, dim, width):
        size = value.shape[dim]
        index = wide_row if dim == 0 else wide_lane
        upper = (index // width) % 2 == 1
        return upper, pltpu.roll(value, width, dim), pltpu.roll(value, size - width, dim)

    def mean_pair(value, dim, width):
        upper, down, up = swap(value, dim, width)
        return 0.5 * (value + jnp.where(upper, down, up))

    def take_upper(value, dim, width):
        upper, _, up = swap(value, dim, width)
        return jnp.where(upper, value, up)

    def take_lower(value, dim, width):
        upper, down, _ = swap(value, dim, width)
        return jnp.where(upper, down, value)

    def coarsen(faces, width):
        result = [[] for _ in range(6)]
        for i in range(len(faces[0]) // 2):
            def both(face):
                return 0.5 * (faces[face][2 * i] + faces[face][2 * i + 1])
            result[0].append(mean_pair(mean_pair(faces[0][2 * i + 1], 0, width), 1, width))
            result[1].append(mean_pair(mean_pair(faces[1][2 * i], 0, width), 1, width))
            result[2].append(mean_pair(take_upper(both(2), 0, width), 1, width))
            result[3].append(mean_pair(take_lower(both(3), 0, width), 1, width))
            result[4].append(mean_pair(take_upper(both(4), 1, width), 0, width))
            result[5].append(mean_pair(take_lower(both(5), 1, width), 0, width))
        return result

    def restrict(field, width):
        return [
            mean_pair(mean_pair(0.5 * (field[2 * i] + field[2 * i + 1]), 0, width), 1, width)
            for i in range(len(field) // 2)
        ]

    def sweep(turn, field, weighted, store, width, copies, keep, between=None):
        count = len(field)
        totals = []
        for i in range(count):
            own = field[i]
            total = keep * own + weighted[i]
            if i < count - 1:
                total = total + store[0, i] * field[i + 1]
            if i > 0:
                total = total + store[1, i] * field[i - 1]
            total = total + store[2, i] * pltpu.roll(own, rows - width, 0)
            total = total + store[3, i] * pltpu.roll(own, width, 0)
            total = total + store[5, i] * pltpu.roll(own, wide - width, 1)
            total = total + store[6, i] * pltpu.roll(own, width, 1)
            totals.append(total)
        if between is not None:
            between()
        wait(copies)
        faces = get_faces(turn, count, width)
        for i in range(count):
            total = totals[i] + store[4, i] * edge_rows(faces, i)
            if i == count - 1:
                total = total + store[0, i] * faces[1]
            if i == 0:
                total = total + store[1, i] * faces[0]
            totals[i] = total
        return totals

    faces0 = [[fine_k[face, i] for i in range(planes)] for face in range(6)]
    build(coeff0, faces0, TAU_FINE, 1)
    weighted0 = [coeff0[7, i] * rhs_wide[i] for i in range(planes)]
    keep = 1.0 - OMEGA
    field = sweep(0, conc, weighted0, coeff0, 1, conc_copies, keep)

    faces1 = []

    def build_middle():
        faces1.extend(coarsen(faces0, 1))
        build(coeff1, faces1, TAU_FINE / 4.0, 2)

    copies = send_faces(2, field, 1)
    field = sweep(2, field, weighted0, coeff0, 1, copies, keep, build_middle)

    def build_low():
        build(coeff2, coarsen(faces1, 2), TAU_FINE / 16.0, 4)

    copies = send_faces(3, field, 1)
    added = sweep(3, field, weighted0, coeff0, 1, copies, -OMEGA, build_low)
    source1 = restrict([added[i] * coeff0[8, i] for i in range(planes)], 1)
    weighted1 = [coeff1[7, i] * source1[i] for i in range(middle)]
    error1 = weighted1
    copies = send_faces(4, error1, 2)
    error1 = sweep(4, error1, weighted1, coeff1, 2, copies, keep)
    copies = send_faces(5, error1, 2)
    added = sweep(5, error1, weighted1, coeff1, 2, copies, -OMEGA)
    source2 = restrict([added[i] * coeff1[8, i] for i in range(middle)], 2)
    low = planes // 4
    weighted2 = [coeff2[7, i] * source2[i] for i in range(low)]
    error2 = weighted2
    turn = 6
    for _ in range(COARSE_SWEEPS - 1):
        copies = send_faces(turn, error2, 4)
        error2 = sweep(turn, error2, weighted2, coeff2, 4, copies, keep)
        turn += 1
    error1 = [error1[i] + error2[i // 2] for i in range(middle)]
    for _ in range(2):
        copies = send_faces(turn, error1, 2)
        error1 = sweep(turn, error1, weighted1, coeff1, 2, copies, keep)
        turn += 1
    field = [field[i] + error1[i // 2] for i in range(planes)]
    for _ in range(2):
        copies = send_faces(turn, field, 1)
        field = sweep(turn, field, weighted0, coeff0, 1, copies, keep)
        turn += 1
    for i in range(planes):
        sol_ref[i] = field[i][:, :lanes]
    for copy in started:
        copy.wait_send()


TURNS = 6 + (COARSE_SWEEPS - 1) + 4


def body(counts, conc, right_side, order_field, grain_ids):
    planes, rows, lanes = conc.shape
    wide = 2 * lanes
    blocks = grain_ids.shape[2]
    vmem = pl.BlockSpec(memory_space=pltpu.VMEM)
    f32, bf16 = jnp.float32, jnp.bfloat16
    dma = pltpu.SemaphoreType.DMA
    out = jax.ShapeDtypeStruct(conc.shape, f32)
    return pl.pallas_call(
        functools.partial(kernel, counts),
        out_shape=(out, out),
        in_specs=[pl.BlockSpec(memory_space=pltpu.HBM)] * 4,
        out_specs=(vmem, vmem),
        scratch_shapes=[
            pltpu.VMEM(conc.shape, f32),
            pltpu.VMEM(conc.shape, f32),
            pltpu.VMEM(order_field.shape, bf16),
            pltpu.VMEM(grain_ids.shape, jnp.int32),
            pltpu.VMEM((planes, rows, wide), f32),
            pltpu.VMEM((2, 2, planes, rows, lanes), f32),
            pltpu.VMEM((2, 2, planes, rows, lanes), f32),
            pltpu.VMEM((TURNS, 4, rows, wide), f32),
            pltpu.VMEM((TURNS, 4, rows, wide), f32),
            pltpu.VMEM((2, SLOTS, planes, lanes), bf16),
            pltpu.VMEM((2, rows, lanes), bf16),
            pltpu.VMEM((2, SLOTS, rows, lanes), bf16),
            pltpu.VMEM((2, SLOTS, planes, lanes), bf16),
            pltpu.VMEM((2, rows, lanes), bf16),
            pltpu.VMEM((2, blocks, lanes), f32),
            pltpu.VMEM((6, blocks, lanes), f32),
            pltpu.VMEM((2, SLOTS, planes, lanes), f32),
            pltpu.VMEM((6, planes, rows, wide), f32),
            pltpu.VMEM((9, planes, rows, wide), f32),
            pltpu.VMEM((9, planes // 2, rows, wide), f32),
            pltpu.VMEM((9, planes // 4, rows, wide), f32),
            dma((TURNS, 4)),
            dma((TURNS, 4)),
            dma((6,)),
            dma((6,)),
            dma((6,)),
            dma((6,)),
            dma((2, 2)),
            dma((2, 2)),
            dma((4,)),
        ],
        compiler_params=pltpu.CompilerParams(
            collective_id=0, has_side_effects=True, vmem_limit_bytes=40 * 1024 * 1024
        ),
    )(conc, right_side, order_field, grain_ids)


def solution(mesh):
    counts = tuple(mesh.shape[axis] for axis in AXES)
    return jax.shard_map(
        functools.partial(body, counts),
        mesh=mesh,
        in_specs=(
            P("gx", "gy", "gz"),
            P("gx", "gy", "gz"),
            P(None, "gx", "gy", "gz"),
            P("gx", "gy", "gz", None),
        ),
        out_specs=(P("gx", "gy", "gz"), P("gx", "gy", "gz")),
        check_vma=False,
    )
```

```python
import functools

import jax
import jax.numpy as jnp
from jax import lax
from jax.experimental import pallas as pl
from jax.experimental.pallas import tpu as pltpu
from jax.sharding import PartitionSpec as P

SLOTS = 8
BRICK = 16
COARSE_SWEEPS = 8
OMEGA = 0.8
TAU_FINE = 256.0
AXES = ("gx", "gy", "gz")
MESH = pl.DeviceIdType.MESH
HIGHEST = lax.Precision.HIGHEST


def kernel(counts, conc_in, rhs_in, order_in, ids_in, sol_ref, mob_ref, conc_ref, rhs_ref, order_ref, ids_ref, rhs_wide,
           deep_send, deep_recv, group_send, group_recv, group_dense, send, recv, order_y, order_z, order_recv_x,
           order_recv_y, order_recv_z, ids_send, ids_recv, rows_ref, fine_k, coeff0, coeff1, coeff2, send_sem,
           recv_sem, order_send_sem, order_recv_sem, ids_send_sem, ids_recv_sem, deep_send_sem, deep_recv_sem, group_send_sem,
           group_recv_sem, load_sem):
    planes, rows, lanes = conc_ref.shape
    wide = 2 * lanes
    half = lanes // 2
    loads = [
        pltpu.make_async_copy(source, dest, load_sem.at[position])
        for position, (source, dest) in enumerate(
            ((ids_in, ids_ref), (order_in, order_ref), (conc_in, conc_ref), (rhs_in, rhs_ref)))
    ]
    for load in loads:
        load.start()
    me = tuple(lax.axis_index(axis) for axis in AXES)

    def beside(dim, sign):
        index = list(me)
        index[dim] = lax.rem(me[dim] + sign + counts[dim], counts[dim])
        return tuple(index)

    targets = [beside(dim, sign) for dim in range(3) for sign in (1, -1)]

    barrier = pltpu.get_barrier_semaphore()
    spots = [(x, y) for x in range(counts[0]) for y in range(counts[1])]
    group = [
        (lax.rem(me[0] - x + counts[0], counts[0]), lax.rem(me[1] - y + counts[1], counts[1]), me[2]) for x, y in spots
    ]
    greeted = targets[4:] + group[1:]
    for target in greeted:
        pl.semaphore_signal(barrier, inc=1, device_id=target, device_id_type=MESH)
    pl.semaphore_wait(barrier, len(greeted))
    for load in loads:
        load.wait()

    row = lax.broadcasted_iota(jnp.int32, (rows, lanes), 0)
    lane = lax.broadcasted_iota(jnp.int32, (rows, lanes), 1)
    zero = jnp.zeros((rows, lanes), jnp.float32)
    started = []

    def start(source, dest, source_sem, dest_sem, face, target=None):
        copy = pltpu.make_async_remote_copy(
            src_ref=source, dst_ref=dest, send_sem=source_sem, recv_sem=dest_sem, device_id=targets[face] if target is None else target,
            device_id_type=MESH)
        copy.start()
        started.append(copy)
        return copy

    def spread_row(line):
        return jnp.broadcast_to(line, (rows, lanes))

    def spread_lane(column):
        return jnp.broadcast_to(column, (rows, lanes))

    wide_row = lax.broadcasted_iota(jnp.int32, (rows, wide), 0)
    wide_lane = lax.broadcasted_iota(jnp.int32, (rows, wide), 1)

    def fold(face, width):
        if width == 1:
            return face
        parity = lax.broadcasted_iota(jnp.int32, (face.shape[0], lanes), 1) % 2
        return jnp.where(parity == 0, face[:, :lanes], face[:, lanes:])

    def unfold(face, width):
        if width == 1:
            return face
        parity = lax.broadcasted_iota(jnp.int32, face.shape, 1) % 2
        own = jnp.where(parity == 0, face, pltpu.roll(face, 1, 1))
        other = jnp.where(parity == 0, pltpu.roll(face, lanes - 1, 1), face)
        return jnp.concatenate([own, other], axis=1)

    def send_faces(turn, field, width):
        count = len(field)
        extent = max(count, 8)
        span = pl.ds(0, wide if width == 1 else lanes)
        copies = []

        def go(face, extent):
            part = (turn, face, pl.ds(0, extent), span)
            copies.append(start(send.at[part], recv.at[part], send_sem.at[turn, face], recv_sem.at[turn, face], face))

        send[turn, 0, :, span] = fold(field[-1], width)
        go(0, rows)
        send[turn, 1, :, span] = fold(field[0], width)
        go(1, rows)
        for face, at in ((2, rows - 1), (3, 0)):
            for i in range(extent):
                send[turn, face, i:i + 1, span] = fold(field[i % count][at:at + 1, :], width)
            go(face, extent)
        return copies

    def get_faces(turn, count, width):
        extent = max(count, 8)
        span = pl.ds(0, wide if width == 1 else lanes)
        whole = [unfold(recv[turn, face, pl.ds(0, rows if face < 2 else extent), span], width) for face in range(4)]
        return whole[:2] + [[face[i:i + 1, :] for i in range(count)] for face in whole[2:]]

    def edge_rows(faces, i):
        return jnp.where(wide_row < rows // 2, jnp.broadcast_to(faces[2][i], (rows, wide)),
                         jnp.broadcast_to(faces[3][i], (rows, wide)))

    low = planes // 4

    def send_group(kind, field):
        packed = field[0]
        for i in range(1, low):
            packed = jnp.where(wide_row % low == i, field[i], packed)
        group_send[kind] = fold(packed, 4)
        copies = []
        for spot in range(1, len(spots)):
            copies.append(start(group_send.at[kind], group_recv.at[kind, spot], group_send_sem.at[kind, spot],
                                group_recv_sem.at[kind, spot], 0, group[spot]))
        group_recv[kind, 0] = group_send[kind]
        return copies

    def get_group(kind):
        for spot, (x, y) in enumerate(spots):
            for i in range(low):
                group_dense[kind, x * low + i, y * low:(y + 1) * low, :] = (
                    group_recv[kind, spot, pl.ds(i, low, stride=low), :])
        return [unfold(group_dense[kind, i], 4) for i in range(low * counts[0])]

    def send_halves(kind, firsts, seconds):
        copies = []
        for face in range(2):
            for i in range(len(firsts)):
                if face == 0:
                    value = jnp.where(lane < half, pltpu.roll(firsts[i], half, 1), seconds[i])
                else:
                    value = jnp.where(lane < half, firsts[i], pltpu.roll(seconds[i], half, 1))
                deep_send[kind, face, i] = value
            part = (kind, face, pl.ds(0, len(firsts)))
            copies.append(start(deep_send.at[part], deep_recv.at[part], deep_send_sem.at[kind, face],
                                deep_recv_sem.at[kind, face], 4 + face))
        return copies

    def widen(kind, firsts, seconds):
        results = [], []
        for i in range(len(firsts)):
            below, above = deep_recv[kind, 0, i], deep_recv[kind, 1, i]
            other = jnp.where(lane < half, above, pltpu.roll(below, half, 1))
            results[0].append(jnp.concatenate([firsts[i], other], axis=1))
            other = jnp.where(lane < half, pltpu.roll(above, half, 1), below)
            results[1].append(jnp.concatenate([seconds[i], other], axis=1))
        return results

    def edge_lanes(minus, plus, i):
        return jnp.where(lane < lanes // 2, spread_lane(minus[:, i:i + 1]), spread_lane(plus[:, i:i + 1]))

    def wait(copies):
        for copy in copies:
            copy.wait_recv()

    ids = ids_ref[0, 0].astype(jnp.float32)
    blocks = ids.shape[0]
    shape = (blocks, lanes)
    chosen = (lax.broadcasted_iota(jnp.int32, shape, 1) // BRICK == lax.broadcasted_iota(jnp.int32, shape, 0))
    chosen = chosen.astype(jnp.float32)
    ids_lane = lax.dot_general(ids, chosen, (((0,), (0,)), ((), ())), precision=HIGHEST,
                               preferred_element_type=jnp.float32)
    ids_slot = lax.dot_general(ids, chosen, (((1,), (0,)), ((), ())), precision=HIGHEST,
                               preferred_element_type=jnp.float32)
    ids_send[0] = ids_lane
    ids_send[1] = ids_slot
    ids_copies = [
        start(ids_send.at[face // 4], ids_recv.at[face], ids_send_sem.at[face], ids_recv_sem.at[face], face)
        for face in range(6)
    ]
    order_copies = [
        start(order_ref.at[:, planes - 1], order_recv_x.at[0], order_send_sem.at[0], order_recv_sem.at[0], 0),
        start(order_ref.at[:, 0], order_recv_x.at[1], order_send_sem.at[1], order_recv_sem.at[1], 1),
    ]

    def pack(i, carry):
        last, first = carry
        for s in range(SLOTS):
            plane = order_ref[s, i].astype(jnp.float32)
            rows_ref[0, s, pl.ds(i, 1), :] = plane[rows - 1:rows, :]
            rows_ref[1, s, pl.ds(i, 1), :] = plane[0:1, :]
            here = lane == s * BRICK + i
            last = jnp.where(here, spread_lane(plane[:, lanes - 1:lanes]), last)
            first = jnp.where(here, spread_lane(plane[:, 0:1]), first)
        return last, first

    last, first = lax.fori_loop(0, planes, pack, (zero, zero))
    for face in range(2):
        order_y[face] = rows_ref[face].astype(jnp.bfloat16)
        order_copies.append(start(order_y.at[face], order_recv_y.at[face], order_send_sem.at[2 + face],
                                  order_recv_sem.at[2 + face], 2 + face))
    for face, value in ((0, last), (1, first)):
        order_z[face] = value.astype(jnp.bfloat16)
        order_copies.append(start(order_z.at[face], order_recv_z.at[face], order_send_sem.at[4 + face],
                                  order_recv_sem.at[4 + face], 4 + face))
    own_conc = [conc_ref[i] for i in range(planes)]
    own_rhs = [rhs_ref[i] for i in range(planes)]
    conc_copies = send_halves(0, own_conc, own_rhs)

    id_lane = lax.broadcasted_iota(jnp.int32, shape, 1)
    ids_next = jnp.where(id_lane == lanes - 1, -1.0, pltpu.roll(ids_lane, lanes - 1, 1))
    ids_before = jnp.where(id_lane == 0, -1.0, pltpu.roll(ids_lane, 1, 1))
    matched, alone = [], []
    for s in range(SLOTS):
        own = jnp.broadcast_to(ids_lane[s:s + 1, :], shape)
        hit = jnp.sum((own == ids_next).astype(jnp.float32), axis=0, keepdims=True)
        matched.append(hit)
        hit = jnp.sum((own == ids_before).astype(jnp.float32), axis=0, keepdims=True)
        alone.append(jnp.where(lax.broadcasted_iota(jnp.int32, (1, lanes), 1) == 0, 0.0, 1.0 - hit))

    def remap(own_ids, other_ids, others):
        result = []
        for s in range(SLOTS):
            value = zero
            for t in range(SLOTS):
                value = jnp.where(spread_row(own_ids[s:s + 1, :]) == spread_row(other_ids[t:t + 1, :]), others[t], value)
            result.append(value)
        return result

    def inside(i, carry):
        above = jnp.minimum(i + 1, planes - 1)
        below = jnp.maximum(i - 1, 0)
        own = [order_ref[s, i].astype(jnp.float32) for s in range(SLOTS)]
        rolled = [pltpu.roll(plane, lanes - 1, 1) for plane in own]
        mapped = remap(ids_lane, ids_next, rolled)
        c = conc_ref[i]
        reaction = c * (1.0 - c)
        total = 1.0 + 8.0 * (reaction * reaction)
        along_y, along_z, shared = zero, zero, zero
        for s in range(SLOTS):
            differ = order_ref[s, above].astype(jnp.float32) - own[s]
            total = total + differ * differ
            differ = order_ref[s, below].astype(jnp.float32) - own[s]
            total = total + differ * differ
            differ = pltpu.roll(own[s], rows - 1, 0) - own[s]
            along_y = along_y + differ * differ
            differ = mapped[s] - own[s]
            square = differ * differ
            along_z = along_z + square
            shared = shared + matched[s] * square
            total = total + alone[s] * (own[s] * own[s])
        along_y = jnp.where(row == rows - 1, 0.0, along_y)
        along_z = jnp.where(lane == lanes - 1, 0.0, along_z)
        total = total + along_y + pltpu.roll(along_y, 1, 0)
        total = total + along_z + pltpu.roll(shared, 1, 1)
        mob_ref[i] = total
        return carry

    lax.fori_loop(0, planes, inside, 0)

    wait(ids_copies)
    wait(order_copies)
    for face, at in ((1, planes - 1), (0, 0)):
        others = [order_recv_x[face, t].astype(jnp.float32) for t in range(SLOTS)]
        mapped = remap(ids_lane, ids_recv[face], others)
        total = mob_ref[at]
        for s in range(SLOTS):
            differ = mapped[s] - order_ref[s, at].astype(jnp.float32)
            total = total + differ * differ
        mob_ref[at] = total
    across = []
    for face in (0, 1):
        others = [order_recv_y[face, t].astype(jnp.float32) for t in range(SLOTS)]
        mapped = remap(ids_lane, ids_recv[2 + face], others)
        total = zero
        for s in range(SLOTS):
            differ = mapped[s] - rows_ref[1 - face, s]
            total = total + differ * differ
        across.append(total)
    ends = []
    for face, own, block in ((0, first, 0), (1, last, blocks - 1)):
        own_ids = spread_row(ids_slot[block:block + 1, :])
        other_block = blocks - 1 - block
        other_ids = spread_row(ids_recv[4 + face, other_block:other_block + 1, :])
        others = order_recv_z[face].astype(jnp.float32)
        value = zero
        for shift in range(0, lanes, BRICK):
            same = own_ids == (pltpu.roll(other_ids, shift, 1) if shift else other_ids)
            value = jnp.where(same, pltpu.roll(others, shift, 1) if shift else others, value)
        differ = value - own
        total = differ * differ
        for shift in (64, 32, 16):
            total = total + pltpu.roll(total, shift, 1)
        ends.append(total)
    mobility = []
    for i in range(planes):
        total = mob_ref[i]
        total = total + jnp.where(row == 0, spread_row(across[0][i:i + 1, :]), 0.0)
        total = total + jnp.where(row == rows - 1, spread_row(across[1][i:i + 1, :]), 0.0)
        at_edge = jnp.logical_or(lane == 0, lane == lanes - 1)
        total = total + jnp.where(at_edge, edge_lanes(ends[0], ends[1], i), 0.0)
        mob_ref[i] = total
        mobility.append(total)
    middle = planes // 2
    copies = send_halves(1, mobility[:middle], mobility[middle:])
    wait(conc_copies)
    conc, rhs = widen(0, own_conc, own_rhs)
    for i in range(planes):
        rhs_wide[i] = rhs[i]
    conc_copies = send_faces(0, conc, 1)
    wait(copies)
    lower, upper = widen(1, mobility[:middle], mobility[middle:])
    mobility = lower + upper
    copies = send_faces(1, mobility, 1)
    for i in range(planes):
        own = mobility[i]
        fine_k[4, i] = 0.5 * (own + pltpu.roll(own, wide - 1, 1))
        fine_k[5, i] = 0.5 * (own + pltpu.roll(own, 1, 1))
    wait(copies)
    faces = get_faces(1, planes, 1)
    for i in range(planes):
        own = mobility[i]
        rims = edge_rows(faces, i)
        fine_k[0, i] = 0.5 * (own + (mobility[i + 1] if i < planes - 1 else faces[1]))
        fine_k[1, i] = 0.5 * (own + (mobility[i - 1] if i > 0 else faces[0]))
        fine_k[2, i] = 0.5 * (own + jnp.where(wide_row == rows - 1, rims, pltpu.roll(own, rows - 1, 0)))
        fine_k[3, i] = 0.5 * (own + jnp.where(wide_row == 0, rims, pltpu.roll(own, 1, 0)))

    def build(store, faces, tau, width):
        for i in range(len(faces[0])):
            k = [face[i] for face in faces]
            diag = 1.0 + tau * (k[0] + k[1] + k[2] + k[3] + k[4] + k[5])
            weight = OMEGA / diag
            scale = tau * weight
            store[0, i] = scale * k[0]
            store[1, i] = scale * k[1]
            top, bottom = wide_row >= rows - width, wide_row < width
            a, b = scale * k[2], scale * k[3]
            store[2, i] = jnp.where(top, 0.0, a)
            store[3, i] = jnp.where(bottom, 0.0, b)
            store[4, i] = jnp.where(top, a, jnp.where(bottom, b, 0.0))
            store[5, i] = scale * k[4]
            store[6, i] = scale * k[5]
            store[7, i] = weight
            store[8, i] = diag * (1.0 / OMEGA)

    def swap(value, dim, width):
        size = value.shape[dim]
        index = wide_row if dim == 0 else wide_lane
        upper = (index // width) % 2 == 1
        return upper, pltpu.roll(value, width, dim), pltpu.roll(value, size - width, dim)

    def mean_pair(value, dim, width):
        upper, down, up = swap(value, dim, width)
        return 0.5 * (value + jnp.where(upper, down, up))

    def take_upper(value, dim, width):
        upper, _, up = swap(value, dim, width)
        return jnp.where(upper, value, up)

    def take_lower(value, dim, width):
        upper, down, _ = swap(value, dim, width)
        return jnp.where(upper, down, value)

    def coarsen(faces, width):
        result = [[] for _ in range(6)]
        for i in range(len(faces[0]) // 2):
            def both(face):
                return 0.5 * (faces[face][2 * i] + faces[face][2 * i + 1])
            result[0].append(mean_pair(mean_pair(faces[0][2 * i + 1], 0, width), 1, width))
            result[1].append(mean_pair(mean_pair(faces[1][2 * i], 0, width), 1, width))
            result[2].append(mean_pair(take_upper(both(2), 0, width), 1, width))
            result[3].append(mean_pair(take_lower(both(3), 0, width), 1, width))
            result[4].append(mean_pair(take_upper(both(4), 1, width), 0, width))
            result[5].append(mean_pair(take_lower(both(5), 1, width), 0, width))
        return result

    def restrict(field, width):
        return [
            mean_pair(mean_pair(0.5 * (field[2 * i] + field[2 * i + 1]), 0, width), 1, width)
            for i in range(len(field) // 2)
        ]

    def sweep(turn, field, weighted, store, width, copies, keep, between=None, faces=None):
        count = len(field)
        totals = []
        for i in range(count):
            own = field[i]
            total = keep * own + weighted[i]
            if i < count - 1:
                total = total + store[0, i] * field[i + 1]
            if i > 0:
                total = total + store[1, i] * field[i - 1]
            total = total + store[2, i] * pltpu.roll(own, rows - width, 0)
            total = total + store[3, i] * pltpu.roll(own, width, 0)
            total = total + store[5, i] * pltpu.roll(own, wide - width, 1)
            total = total + store[6, i] * pltpu.roll(own, width, 1)
            totals.append(total)
        if between is not None:
            between()
        wait(copies)
        if faces is None:
            faces = get_faces(turn, count, width)
        for i in range(count):
            total = totals[i] + store[4, i] * edge_rows(faces, i)
            if i == count - 1:
                total = total + store[0, i] * faces[1]
            if i == 0:
                total = total + store[1, i] * faces[0]
            totals[i] = total
        return totals

    faces0 = [[fine_k[face, i] for i in range(planes)] for face in range(6)]
    build(coeff0, faces0, TAU_FINE, 1)
    weighted0 = [coeff0[7, i] * rhs_wide[i] for i in range(planes)]
    keep = 1.0 - OMEGA
    field = sweep(0, conc, weighted0, coeff0, 1, conc_copies, keep)

    faces1 = []

    def build_middle():
        faces1.extend(coarsen(faces0, 1))
        build(coeff1, faces1, TAU_FINE / 4.0, 2)

    copies = send_faces(2, field, 1)
    field = sweep(2, field, weighted0, coeff0, 1, copies, keep, build_middle)

    low_copies = []

    def share_low():
        low_faces = coarsen(faces1, 2)
        for dim in range(3):
            low_copies.extend(send_group(dim, low_faces[2 * dim]))

    span = low * counts[0]
    depth = low * counts[1]

    def build_low():
        wait(low_copies)
        along_x, along_y, along_z = get_group(0), get_group(1), get_group(2)
        tau = TAU_FINE / 16.0
        for i in range(span):
            k = [along_x[i], along_x[i - 1], along_y[i], pltpu.roll(along_y[i], 1, 0), along_z[i],
                 pltpu.roll(along_z[i], 4, 1)]
            weight = OMEGA / (1.0 + tau * (k[0] + k[1] + k[2] + k[3] + k[4] + k[5]))
            scale = tau * weight
            for face in range(6):
                coeff2[face, i] = scale * k[face]
            coeff2[6, i] = weight

    def low_sweep(field, weighted):
        result = []
        for i in range(span):
            own = field[i]
            total = keep * own + weighted[i]
            total = total + coeff2[0, i] * field[(i + 1) % span]
            total = total + coeff2[1, i] * field[i - 1]
            total = total + coeff2[2, i] * pltpu.roll(own, depth - 1, 0)
            total = total + coeff2[3, i] * pltpu.roll(own, 1, 0)
            total = total + coeff2[4, i] * pltpu.roll(own, wide - 4, 1)
            total = total + coeff2[5, i] * pltpu.roll(own, 4, 1)
            result.append(total)
        return result

    copies = send_faces(3, field, 1)
    added = sweep(3, field, weighted0, coeff0, 1, copies, -OMEGA, share_low)
    source1 = restrict([added[i] * coeff0[8, i] for i in range(planes)], 1)
    weighted1 = [coeff1[7, i] * source1[i] for i in range(middle)]
    error1 = weighted1
    copies = send_faces(4, error1, 2)
    error1 = sweep(4, error1, weighted1, coeff1, 2, copies, keep)
    copies = send_faces(5, error1, 2)
    added = sweep(5, error1, weighted1, coeff1, 2, copies, -OMEGA, build_low)
    source2 = restrict([added[i] * coeff1[8, i] for i in range(middle)], 2)
    wait(send_group(3, source2))
    source2 = get_group(3)
    weighted2 = [coeff2[6, i] * source2[i] for i in range(span)]
    error2 = weighted2
    for _ in range(COARSE_SWEEPS - 1):
        error2 = low_sweep(error2, weighted2)

    def spread(plane):
        value = jnp.broadcast_to(plane[0:1, :], (rows, wide))
        for j in range(1, low):
            value = jnp.where(wide_row >= j * (rows // low), jnp.broadcast_to(plane[j:j + 1, :], (rows, wide)), value)
        return value

    below, above = span - 1, low % span
    left, right = depth - 1, low % depth
    old = get_faces(5, middle, 2)
    faces = [old[0] + spread(error2[below]), old[1] + spread(error2[above]),
             [old[2][i] + error2[i // 2][left:left + 1, :] for i in range(middle)],
             [old[3][i] + error2[i // 2][right:right + 1, :] for i in range(middle)]]
    spread2 = [spread(error2[i]) for i in range(low)]
    error1 = [error1[i] + spread2[i // 2] for i in range(middle)]
    error1 = sweep(5, error1, weighted1, coeff1, 2, [], keep, faces=faces)
    turn = 6
    copies = send_faces(turn, error1, 2)
    error1 = sweep(turn, error1, weighted1, coeff1, 2, copies, keep)
    turn += 1
    field = [field[i] + error1[i // 2] for i in range(planes)]
    for _ in range(2):
        copies = send_faces(turn, field, 1)
        field = sweep(turn, field, weighted0, coeff0, 1, copies, keep)
        turn += 1
    for i in range(planes):
        sol_ref[i] = field[i][:, :lanes]
    for copy in started:
        copy.wait_send()


TURNS = 9


def body(counts, conc, right_side, order_field, grain_ids):
    planes, rows, lanes = conc.shape
    wide = 2 * lanes
    blocks = grain_ids.shape[2]
    vmem = pl.BlockSpec(memory_space=pltpu.VMEM)
    f32, bf16 = jnp.float32, jnp.bfloat16
    dma = pltpu.SemaphoreType.DMA
    out = jax.ShapeDtypeStruct(conc.shape, f32)
    return pl.pallas_call(
        functools.partial(kernel, counts),
        out_shape=(out, out),
        in_specs=[pl.BlockSpec(memory_space=pltpu.HBM)] * 4,
        out_specs=(vmem, vmem),
        scratch_shapes=[
            pltpu.VMEM(conc.shape, f32),
            pltpu.VMEM(conc.shape, f32),
            pltpu.VMEM(order_field.shape, bf16),
            pltpu.VMEM(grain_ids.shape, jnp.int32),
            pltpu.VMEM((planes, rows, wide), f32),
            pltpu.VMEM((2, 2, planes, rows, lanes), f32),
            pltpu.VMEM((2, 2, planes, rows, lanes), f32),
            pltpu.VMEM((4, rows, lanes), f32),
            pltpu.VMEM((4, counts[0] * counts[1], rows, lanes), f32),
            pltpu.VMEM((4, planes // 4 * counts[0], rows // 4 * counts[1], lanes), f32),
            pltpu.VMEM((TURNS, 4, rows, wide), f32),
            pltpu.VMEM((TURNS, 4, rows, wide), f32),
            pltpu.VMEM((2, SLOTS, planes, lanes), bf16),
            pltpu.VMEM((2, rows, lanes), bf16),
            pltpu.VMEM((2, SLOTS, rows, lanes), bf16),
            pltpu.VMEM((2, SLOTS, planes, lanes), bf16),
            pltpu.VMEM((2, rows, lanes), bf16),
            pltpu.VMEM((2, blocks, lanes), f32),
            pltpu.VMEM((6, blocks, lanes), f32),
            pltpu.VMEM((2, SLOTS, planes, lanes), f32),
            pltpu.VMEM((6, planes, rows, wide), f32),
            pltpu.VMEM((9, planes, rows, wide), f32),
            pltpu.VMEM((9, planes // 2, rows, wide), f32),
            pltpu.VMEM((7, planes // 4 * counts[0], rows // 4 * counts[1], wide), f32),
            dma((TURNS, 4)),
            dma((TURNS, 4)),
            dma((6,)),
            dma((6,)),
            dma((6,)),
            dma((6,)),
            dma((2, 2)),
            dma((2, 2)),
            dma((4, counts[0] * counts[1])),
            dma((4, counts[0] * counts[1])),
            dma((4,)),
        ],
        compiler_params=pltpu.CompilerParams(
            collective_id=0, has_side_effects=True, vmem_limit_bytes=62 * 1024 * 1024
        ),
    )(conc, right_side, order_field, grain_ids)


def solution(mesh):
    counts = tuple(mesh.shape[axis] for axis in AXES)
    return jax.shard_map(
        functools.partial(body, counts),
        mesh=mesh,
        in_specs=(
            P("gx", "gy", "gz"),
            P("gx", "gy", "gz"),
            P(None, "gx", "gy", "gz"),
            P("gx", "gy", "gz", None),
        ),
        out_specs=(P("gx", "gy", "gz"), P("gx", "gy", "gz")),
        check_vma=False,
    )
```

```python
import functools

import jax
import jax.numpy as jnp
from jax import lax
from jax.experimental import pallas as pl
from jax.experimental.pallas import tpu as pltpu
from jax.sharding import PartitionSpec as P

SLOTS = 8
BRICK = 16
COARSE_SWEEPS = 8
OMEGA = 0.8
TAU_FINE = 256.0
AXES = ("gx", "gy", "gz")
MESH = pl.DeviceIdType.MESH
HIGHEST = lax.Precision.HIGHEST


def kernel(counts, conc_in, rhs_in, order_in, ids_in, sol_ref, mob_ref, conc_ref, rhs_ref, order_ref, ids_ref, rhs_wide,
           deep_send, deep_recv, group_send, group_recv, group_dense, corner_recv, send, recv, order_y, order_z, order_recv_x,
           order_recv_y, order_recv_z, ids_send, ids_recv, rows_ref, fine_k, coeff0, coeff1, coeff2, send_sem,
           recv_sem, order_send_sem, order_recv_sem, ids_send_sem, ids_recv_sem, deep_send_sem, deep_recv_sem, group_send_sem,
           group_recv_sem, corner_send_sem, corner_recv_sem, load_sem):
    planes, rows, lanes = conc_ref.shape
    wide = 2 * lanes
    half = lanes // 2
    loads = [
        pltpu.make_async_copy(source, dest, load_sem.at[position])
        for position, (source, dest) in enumerate(
            ((ids_in, ids_ref), (order_in, order_ref), (conc_in, conc_ref), (rhs_in, rhs_ref)))
    ]
    for load in loads:
        load.start()
    me = tuple(lax.axis_index(axis) for axis in AXES)

    def beside(dim, sign):
        index = list(me)
        index[dim] = lax.rem(me[dim] + sign + counts[dim], counts[dim])
        return tuple(index)

    targets = [beside(dim, sign) for dim in range(3) for sign in (1, -1)]

    barrier = pltpu.get_barrier_semaphore()
    spots = [(x, y) for x in range(counts[0]) for y in range(counts[1])]
    group = [
        (lax.rem(me[0] - x + counts[0], counts[0]), lax.rem(me[1] - y + counts[1], counts[1]), me[2]) for x, y in spots
    ]
    corners = [
        (face, side, targets[face][:2] + (targets[4 + side][2],)) for face in range(4) for side in range(2)
    ]
    greeted = targets[4:] + group[1:] + [target for _, _, target in corners]
    for target in greeted:
        pl.semaphore_signal(barrier, inc=1, device_id=target, device_id_type=MESH)
    pl.semaphore_wait(barrier, len(greeted))
    for load in loads:
        load.wait()

    row = lax.broadcasted_iota(jnp.int32, (rows, lanes), 0)
    lane = lax.broadcasted_iota(jnp.int32, (rows, lanes), 1)
    zero = jnp.zeros((rows, lanes), jnp.float32)
    started = []

    def start(source, dest, source_sem, dest_sem, face, target=None):
        copy = pltpu.make_async_remote_copy(
            src_ref=source, dst_ref=dest, send_sem=source_sem, recv_sem=dest_sem, device_id=targets[face] if target is None else target,
            device_id_type=MESH)
        copy.start()
        started.append(copy)
        return copy

    def spread_row(line):
        return jnp.broadcast_to(line, (rows, lanes))

    def spread_lane(column):
        return jnp.broadcast_to(column, (rows, lanes))

    wide_row = lax.broadcasted_iota(jnp.int32, (rows, wide), 0)
    wide_lane = lax.broadcasted_iota(jnp.int32, (rows, wide), 1)

    def fold(face, width):
        if width == 1:
            return face
        parity = lax.broadcasted_iota(jnp.int32, (face.shape[0], lanes), 1) % 2
        return jnp.where(parity == 0, face[:, :lanes], face[:, lanes:])

    def unfold(face, width):
        if width == 1:
            return face
        parity = lax.broadcasted_iota(jnp.int32, face.shape, 1) % 2
        own = jnp.where(parity == 0, face, pltpu.roll(face, 1, 1))
        other = jnp.where(parity == 0, pltpu.roll(face, lanes - 1, 1), face)
        return jnp.concatenate([own, other], axis=1)

    def send_faces(turn, field, width):
        count = len(field)
        extent = max(count, 8)
        span = pl.ds(0, wide if width == 1 else lanes)
        copies = []

        def go(face, extent):
            part = (turn, face, pl.ds(0, extent), span)
            copies.append(start(send.at[part], recv.at[part], send_sem.at[turn, face], recv_sem.at[turn, face], face))

        send[turn, 0, :, span] = fold(field[-1], width)
        go(0, rows)
        send[turn, 1, :, span] = fold(field[0], width)
        go(1, rows)
        for face, at in ((2, rows - 1), (3, 0)):
            for i in range(extent):
                send[turn, face, i:i + 1, span] = fold(field[i % count][at:at + 1, :], width)
            go(face, extent)
        return copies

    def get_faces(turn, count, width):
        extent = max(count, 8)
        span = pl.ds(0, wide if width == 1 else lanes)
        whole = [unfold(recv[turn, face, pl.ds(0, rows if face < 2 else extent), span], width) for face in range(4)]
        return whole[:2] + [[face[i:i + 1, :] for i in range(count)] for face in whole[2:]]

    def edge_rows(faces, i):
        return jnp.where(wide_row < rows // 2, jnp.broadcast_to(faces[2][i], (rows, wide)),
                         jnp.broadcast_to(faces[3][i], (rows, wide)))

    low = planes // 4

    def send_group(kind, field):
        packed = field[0]
        for i in range(1, low):
            packed = jnp.where(wide_row % low == i, field[i], packed)
        group_send[kind] = fold(packed, 4)
        copies = []
        for spot in range(1, len(spots)):
            copies.append(start(group_send.at[kind], group_recv.at[kind, spot], group_send_sem.at[kind, spot],
                                group_recv_sem.at[kind, spot], 0, group[spot]))
        group_recv[kind, 0] = group_send[kind]
        return copies

    def get_group(kind):
        for spot, (x, y) in enumerate(spots):
            for i in range(low):
                group_dense[kind, x * low + i, y * low:(y + 1) * low, :] = (
                    group_recv[kind, spot, pl.ds(i, low, stride=low), :])
        return [unfold(group_dense[kind, i], 4) for i in range(low * counts[0])]

    def send_halves(kind, firsts, seconds):
        copies = []
        for face in range(2):
            for i in range(len(firsts)):
                if face == 0:
                    value = jnp.where(lane < half, pltpu.roll(firsts[i], half, 1), seconds[i])
                else:
                    value = jnp.where(lane < half, firsts[i], pltpu.roll(seconds[i], half, 1))
                deep_send[kind, face, i] = value
            part = (kind, face, pl.ds(0, len(firsts)))
            copies.append(start(deep_send.at[part], deep_recv.at[part], deep_send_sem.at[kind, face],
                                deep_recv_sem.at[kind, face], 4 + face))
        return copies

    def widen(kind, firsts, seconds):
        results = [], []
        for i in range(len(firsts)):
            below, above = deep_recv[kind, 0, i], deep_recv[kind, 1, i]
            other = jnp.where(lane < half, above, pltpu.roll(below, half, 1))
            results[0].append(jnp.concatenate([firsts[i], other], axis=1))
            other = jnp.where(lane < half, pltpu.roll(above, half, 1), below)
            results[1].append(jnp.concatenate([seconds[i], other], axis=1))
        return results

    def edge_lanes(minus, plus, i):
        return jnp.where(lane < lanes // 2, spread_lane(minus[:, i:i + 1]), spread_lane(plus[:, i:i + 1]))

    def wait(copies):
        for copy in copies:
            copy.wait_recv()

    ids = ids_ref[0, 0].astype(jnp.float32)
    blocks = ids.shape[0]
    shape = (blocks, lanes)
    chosen = (lax.broadcasted_iota(jnp.int32, shape, 1) // BRICK == lax.broadcasted_iota(jnp.int32, shape, 0))
    chosen = chosen.astype(jnp.float32)
    ids_lane = lax.dot_general(ids, chosen, (((0,), (0,)), ((), ())), precision=HIGHEST,
                               preferred_element_type=jnp.float32)
    ids_slot = lax.dot_general(ids, chosen, (((1,), (0,)), ((), ())), precision=HIGHEST,
                               preferred_element_type=jnp.float32)
    ids_send[0] = ids_lane
    ids_send[1] = ids_slot
    ids_copies = [
        start(ids_send.at[face // 4], ids_recv.at[face], ids_send_sem.at[face], ids_recv_sem.at[face], face)
        for face in range(6)
    ]
    order_copies = [
        start(order_ref.at[:, planes - 1], order_recv_x.at[0], order_send_sem.at[0], order_recv_sem.at[0], 0),
        start(order_ref.at[:, 0], order_recv_x.at[1], order_send_sem.at[1], order_recv_sem.at[1], 1),
    ]

    def pack(i, carry):
        last, first = carry
        for s in range(SLOTS):
            plane = order_ref[s, i].astype(jnp.float32)
            rows_ref[0, s, pl.ds(i, 1), :] = plane[rows - 1:rows, :]
            rows_ref[1, s, pl.ds(i, 1), :] = plane[0:1, :]
            here = lane == s * BRICK + i
            last = jnp.where(here, spread_lane(plane[:, lanes - 1:lanes]), last)
            first = jnp.where(here, spread_lane(plane[:, 0:1]), first)
        return last, first

    last, first = lax.fori_loop(0, planes, pack, (zero, zero))
    for face in range(2):
        order_y[face] = rows_ref[face].astype(jnp.bfloat16)
        order_copies.append(start(order_y.at[face], order_recv_y.at[face], order_send_sem.at[2 + face],
                                  order_recv_sem.at[2 + face], 2 + face))
    for face, value in ((0, last), (1, first)):
        order_z[face] = value.astype(jnp.bfloat16)
        order_copies.append(start(order_z.at[face], order_recv_z.at[face], order_send_sem.at[4 + face],
                                  order_recv_sem.at[4 + face], 4 + face))
    own_conc = [conc_ref[i] for i in range(planes)]
    own_rhs = [rhs_ref[i] for i in range(planes)]
    conc_copies = send_halves(0, own_conc, own_rhs)

    id_lane = lax.broadcasted_iota(jnp.int32, shape, 1)
    ids_next = jnp.where(id_lane == lanes - 1, -1.0, pltpu.roll(ids_lane, lanes - 1, 1))
    ids_before = jnp.where(id_lane == 0, -1.0, pltpu.roll(ids_lane, 1, 1))
    matched, alone = [], []
    for s in range(SLOTS):
        own = jnp.broadcast_to(ids_lane[s:s + 1, :], shape)
        hit = jnp.sum((own == ids_next).astype(jnp.float32), axis=0, keepdims=True)
        matched.append(hit)
        hit = jnp.sum((own == ids_before).astype(jnp.float32), axis=0, keepdims=True)
        alone.append(jnp.where(lax.broadcasted_iota(jnp.int32, (1, lanes), 1) == 0, 0.0, 1.0 - hit))

    def remap(own_ids, other_ids, others):
        result = []
        for s in range(SLOTS):
            value = zero
            for t in range(SLOTS):
                value = jnp.where(spread_row(own_ids[s:s + 1, :]) == spread_row(other_ids[t:t + 1, :]), others[t], value)
            result.append(value)
        return result

    def inside(i, carry):
        above = jnp.minimum(i + 1, planes - 1)
        below = jnp.maximum(i - 1, 0)
        own = [order_ref[s, i].astype(jnp.float32) for s in range(SLOTS)]
        rolled = [pltpu.roll(plane, lanes - 1, 1) for plane in own]
        mapped = remap(ids_lane, ids_next, rolled)
        c = conc_ref[i]
        reaction = c * (1.0 - c)
        total = 1.0 + 8.0 * (reaction * reaction)
        along_y, along_z, shared = zero, zero, zero
        for s in range(SLOTS):
            differ = order_ref[s, above].astype(jnp.float32) - own[s]
            total = total + differ * differ
            differ = order_ref[s, below].astype(jnp.float32) - own[s]
            total = total + differ * differ
            differ = pltpu.roll(own[s], rows - 1, 0) - own[s]
            along_y = along_y + differ * differ
            differ = mapped[s] - own[s]
            square = differ * differ
            along_z = along_z + square
            shared = shared + matched[s] * square
            total = total + alone[s] * (own[s] * own[s])
        along_y = jnp.where(row == rows - 1, 0.0, along_y)
        along_z = jnp.where(lane == lanes - 1, 0.0, along_z)
        total = total + along_y + pltpu.roll(along_y, 1, 0)
        total = total + along_z + pltpu.roll(shared, 1, 1)
        mob_ref[i] = total
        return carry

    lax.fori_loop(0, planes, inside, 0)

    wait(ids_copies)
    wait(order_copies)
    for face, at in ((1, planes - 1), (0, 0)):
        others = [order_recv_x[face, t].astype(jnp.float32) for t in range(SLOTS)]
        mapped = remap(ids_lane, ids_recv[face], others)
        total = mob_ref[at]
        for s in range(SLOTS):
            differ = mapped[s] - order_ref[s, at].astype(jnp.float32)
            total = total + differ * differ
        mob_ref[at] = total
    across = []
    for face in (0, 1):
        others = [order_recv_y[face, t].astype(jnp.float32) for t in range(SLOTS)]
        mapped = remap(ids_lane, ids_recv[2 + face], others)
        total = zero
        for s in range(SLOTS):
            differ = mapped[s] - rows_ref[1 - face, s]
            total = total + differ * differ
        across.append(total)
    ends = []
    for face, own, block in ((0, first, 0), (1, last, blocks - 1)):
        own_ids = spread_row(ids_slot[block:block + 1, :])
        other_block = blocks - 1 - block
        other_ids = spread_row(ids_recv[4 + face, other_block:other_block + 1, :])
        others = order_recv_z[face].astype(jnp.float32)
        value = zero
        for shift in range(0, lanes, BRICK):
            same = own_ids == (pltpu.roll(other_ids, shift, 1) if shift else other_ids)
            value = jnp.where(same, pltpu.roll(others, shift, 1) if shift else others, value)
        differ = value - own
        total = differ * differ
        for shift in (64, 32, 16):
            total = total + pltpu.roll(total, shift, 1)
        ends.append(total)
    mobility = []
    for i in range(planes):
        total = mob_ref[i]
        total = total + jnp.where(row == 0, spread_row(across[0][i:i + 1, :]), 0.0)
        total = total + jnp.where(row == rows - 1, spread_row(across[1][i:i + 1, :]), 0.0)
        at_edge = jnp.logical_or(lane == 0, lane == lanes - 1)
        total = total + jnp.where(at_edge, edge_lanes(ends[0], ends[1], i), 0.0)
        mob_ref[i] = total
        mobility.append(total)
    middle = planes // 2
    edge = pl.ds(0, rows), pl.ds(0, lanes)
    send[(1, 0) + edge] = mobility[-1]
    send[(1, 1) + edge] = mobility[0]
    for face, at in ((2, rows - 1), (3, 0)):
        for i in range(planes):
            send[1, face, i:i + 1, pl.ds(0, lanes)] = mobility[i][at:at + 1, :]
    face_copies = []
    for face, side, target in corners:
        face_copies.append(start(send.at[(1, face) + edge], corner_recv.at[face, side], corner_send_sem.at[face, side],
                                 corner_recv_sem.at[face, side], 0, target))
    for face in range(4):
        face_copies.append(start(send.at[(1, face) + edge], recv.at[(1, face) + edge], send_sem.at[1, face],
                                 recv_sem.at[1, face], face))
    copies = send_halves(1, mobility[:middle], mobility[middle:])
    wait(conc_copies)
    conc, rhs = widen(0, own_conc, own_rhs)
    for i in range(planes):
        rhs_wide[i] = rhs[i]
    conc_copies = send_faces(0, conc, 1)
    wait(copies)
    lower, upper = widen(1, mobility[:middle], mobility[middle:])
    mobility = lower + upper
    for i in range(planes):
        own = mobility[i]
        fine_k[4, i] = 0.5 * (own + pltpu.roll(own, wide - 1, 1))
        fine_k[5, i] = 0.5 * (own + pltpu.roll(own, 1, 1))
    wait(face_copies)
    faces = [
        jnp.concatenate([recv[(1, face) + edge], jnp.where(lane < half, corner_recv[face, 1], corner_recv[face, 0])],
                        axis=1) for face in range(4)
    ]
    faces = faces[:2] + [[face[i:i + 1, :] for i in range(planes)] for face in faces[2:]]
    for i in range(planes):
        own = mobility[i]
        rims = edge_rows(faces, i)
        fine_k[0, i] = 0.5 * (own + (mobility[i + 1] if i < planes - 1 else faces[1]))
        fine_k[1, i] = 0.5 * (own + (mobility[i - 1] if i > 0 else faces[0]))
        fine_k[2, i] = 0.5 * (own + jnp.where(wide_row == rows - 1, rims, pltpu.roll(own, rows - 1, 0)))
        fine_k[3, i] = 0.5 * (own + jnp.where(wide_row == 0, rims, pltpu.roll(own, 1, 0)))

    def build(store, faces, tau, width):
        for i in range(len(faces[0])):
            k = [face[i] for face in faces]
            diag = 1.0 + tau * (k[0] + k[1] + k[2] + k[3] + k[4] + k[5])
            weight = OMEGA / diag
            scale = tau * weight
            store[0, i] = scale * k[0]
            store[1, i] = scale * k[1]
            top, bottom = wide_row >= rows - width, wide_row < width
            a, b = scale * k[2], scale * k[3]
            store[2, i] = jnp.where(top, 0.0, a)
            store[3, i] = jnp.where(bottom, 0.0, b)
            store[4, i] = jnp.where(top, a, jnp.where(bottom, b, 0.0))
            store[5, i] = scale * k[4]
            store[6, i] = scale * k[5]
            store[7, i] = weight
            store[8, i] = diag * (1.0 / OMEGA)

    def swap(value, dim, width):
        size = value.shape[dim]
        index = wide_row if dim == 0 else wide_lane
        upper = (index // width) % 2 == 1
        return upper, pltpu.roll(value, width, dim), pltpu.roll(value, size - width, dim)

    def mean_pair(value, dim, width):
        upper, down, up = swap(value, dim, width)
        return 0.5 * (value + jnp.where(upper, down, up))

    def take_upper(value, dim, width):
        upper, _, up = swap(value, dim, width)
        return jnp.where(upper, value, up)

    def take_lower(value, dim, width):
        upper, down, _ = swap(value, dim, width)
        return jnp.where(upper, down, value)

    def coarsen(faces, width):
        result = [[] for _ in range(6)]
        for i in range(len(faces[0]) // 2):
            def both(face):
                return 0.5 * (faces[face][2 * i] + faces[face][2 * i + 1])
            result[0].append(mean_pair(mean_pair(faces[0][2 * i + 1], 0, width), 1, width))
            result[1].append(mean_pair(mean_pair(faces[1][2 * i], 0, width), 1, width))
            result[2].append(mean_pair(take_upper(both(2), 0, width), 1, width))
            result[3].append(mean_pair(take_lower(both(3), 0, width), 1, width))
            result[4].append(mean_pair(take_upper(both(4), 1, width), 0, width))
            result[5].append(mean_pair(take_lower(both(5), 1, width), 0, width))
        return result

    def restrict(field, width):
        return [
            mean_pair(mean_pair(0.5 * (field[2 * i] + field[2 * i + 1]), 0, width), 1, width)
            for i in range(len(field) // 2)
        ]

    def sweep(turn, field, weighted, store, width, copies, keep, between=None, faces=None):
        count = len(field)
        totals = []
        for i in range(count):
            own = field[i]
            total = keep * own + weighted[i]
            if i < count - 1:
                total = total + store[0, i] * field[i + 1]
            if i > 0:
                total = total + store[1, i] * field[i - 1]
            total = total + store[2, i] * pltpu.roll(own, rows - width, 0)
            total = total + store[3, i] * pltpu.roll(own, width, 0)
            total = total + store[5, i] * pltpu.roll(own, wide - width, 1)
            total = total + store[6, i] * pltpu.roll(own, width, 1)
            totals.append(total)
        if between is not None:
            between()
        wait(copies)
        if faces is None:
            faces = get_faces(turn, count, width)
        for i in range(count):
            total = totals[i] + store[4, i] * edge_rows(faces, i)
            if i == count - 1:
                total = total + store[0, i] * faces[1]
            if i == 0:
                total = total + store[1, i] * faces[0]
            totals[i] = total
        return totals

    faces0 = [[fine_k[face, i] for i in range(planes)] for face in range(6)]
    build(coeff0, faces0, TAU_FINE, 1)
    weighted0 = [coeff0[7, i] * rhs_wide[i] for i in range(planes)]
    keep = 1.0 - OMEGA
    field = sweep(0, conc, weighted0, coeff0, 1, conc_copies, keep)

    faces1 = []

    def build_middle():
        faces1.extend(coarsen(faces0, 1))
        build(coeff1, faces1, TAU_FINE / 4.0, 2)

    copies = send_faces(2, field, 1)
    field = sweep(2, field, weighted0, coeff0, 1, copies, keep, build_middle)

    low_copies = []

    def share_low():
        low_faces = coarsen(faces1, 2)
        for dim in range(3):
            low_copies.extend(send_group(dim, low_faces[2 * dim]))

    span = low * counts[0]
    depth = low * counts[1]

    def build_low():
        wait(low_copies)
        along_x, along_y, along_z = get_group(0), get_group(1), get_group(2)
        tau = TAU_FINE / 16.0
        for i in range(span):
            k = [along_x[i], along_x[i - 1], along_y[i], pltpu.roll(along_y[i], 1, 0), along_z[i],
                 pltpu.roll(along_z[i], 4, 1)]
            weight = OMEGA / (1.0 + tau * (k[0] + k[1] + k[2] + k[3] + k[4] + k[5]))
            scale = tau * weight
            for face in range(6):
                coeff2[face, i] = scale * k[face]
            coeff2[6, i] = weight

    def low_sweep(field, weighted):
        result = []
        for i in range(span):
            own = field[i]
            total = keep * own + weighted[i]
            total = total + coeff2[0, i] * field[(i + 1) % span]
            total = total + coeff2[1, i] * field[i - 1]
            total = total + coeff2[2, i] * pltpu.roll(own, depth - 1, 0)
            total = total + coeff2[3, i] * pltpu.roll(own, 1, 0)
            total = total + coeff2[4, i] * pltpu.roll(own, wide - 4, 1)
            total = total + coeff2[5, i] * pltpu.roll(own, 4, 1)
            result.append(total)
        return result

    copies = send_faces(3, field, 1)
    added = sweep(3, field, weighted0, coeff0, 1, copies, -OMEGA, share_low)
    source1 = restrict([added[i] * coeff0[8, i] for i in range(planes)], 1)
    weighted1 = [coeff1[7, i] * source1[i] for i in range(middle)]
    error1 = weighted1
    copies = send_faces(4, error1, 2)
    error1 = sweep(4, error1, weighted1, coeff1, 2, copies, keep)
    copies = send_faces(5, error1, 2)
    added = sweep(5, error1, weighted1, coeff1, 2, copies, -OMEGA, build_low)
    source2 = restrict([added[i] * coeff1[8, i] for i in range(middle)], 2)
    wait(send_group(3, source2))
    source2 = get_group(3)
    weighted2 = [coeff2[6, i] * source2[i] for i in range(span)]
    error2 = weighted2
    for _ in range(COARSE_SWEEPS - 1):
        error2 = low_sweep(error2, weighted2)

    def spread(plane):
        value = jnp.broadcast_to(plane[0:1, :], (rows, wide))
        for j in range(1, low):
            value = jnp.where(wide_row >= j * (rows // low), jnp.broadcast_to(plane[j:j + 1, :], (rows, wide)), value)
        return value

    below, above = span - 1, low % span
    left, right = depth - 1, low % depth
    old = get_faces(5, middle, 2)
    faces = [old[0] + spread(error2[below]), old[1] + spread(error2[above]),
             [old[2][i] + error2[i // 2][left:left + 1, :] for i in range(middle)],
             [old[3][i] + error2[i // 2][right:right + 1, :] for i in range(middle)]]
    spread2 = [spread(error2[i]) for i in range(low)]
    error1 = [error1[i] + spread2[i // 2] for i in range(middle)]
    error1 = sweep(5, error1, weighted1, coeff1, 2, [], keep, faces=faces)
    turn = 6
    copies = send_faces(turn, error1, 2)
    error1 = sweep(turn, error1, weighted1, coeff1, 2, copies, keep)
    turn += 1
    field = [field[i] + error1[i // 2] for i in range(planes)]
    for _ in range(2):
        copies = send_faces(turn, field, 1)
        field = sweep(turn, field, weighted0, coeff0, 1, copies, keep)
        turn += 1
    for i in range(planes):
        sol_ref[i] = field[i][:, :lanes]
    for copy in started:
        copy.wait_send()


TURNS = 9


def body(counts, conc, right_side, order_field, grain_ids):
    planes, rows, lanes = conc.shape
    wide = 2 * lanes
    blocks = grain_ids.shape[2]
    vmem = pl.BlockSpec(memory_space=pltpu.VMEM)
    f32, bf16 = jnp.float32, jnp.bfloat16
    dma = pltpu.SemaphoreType.DMA
    out = jax.ShapeDtypeStruct(conc.shape, f32)
    return pl.pallas_call(
        functools.partial(kernel, counts),
        out_shape=(out, out),
        in_specs=[pl.BlockSpec(memory_space=pltpu.HBM)] * 4,
        out_specs=(vmem, vmem),
        scratch_shapes=[
            pltpu.VMEM(conc.shape, f32),
            pltpu.VMEM(conc.shape, f32),
            pltpu.VMEM(order_field.shape, bf16),
            pltpu.VMEM(grain_ids.shape, jnp.int32),
            pltpu.VMEM((planes, rows, wide), f32),
            pltpu.VMEM((2, 2, planes, rows, lanes), f32),
            pltpu.VMEM((2, 2, planes, rows, lanes), f32),
            pltpu.VMEM((4, rows, lanes), f32),
            pltpu.VMEM((4, counts[0] * counts[1], rows, lanes), f32),
            pltpu.VMEM((4, planes // 4 * counts[0], rows // 4 * counts[1], lanes), f32),
            pltpu.VMEM((4, 2, rows, lanes), f32),
            pltpu.VMEM((TURNS, 4, rows, wide), f32),
            pltpu.VMEM((TURNS, 4, rows, wide), f32),
            pltpu.VMEM((2, SLOTS, planes, lanes), bf16),
            pltpu.VMEM((2, rows, lanes), bf16),
            pltpu.VMEM((2, SLOTS, rows, lanes), bf16),
            pltpu.VMEM((2, SLOTS, planes, lanes), bf16),
            pltpu.VMEM((2, rows, lanes), bf16),
            pltpu.VMEM((2, blocks, lanes), f32),
            pltpu.VMEM((6, blocks, lanes), f32),
            pltpu.VMEM((2, SLOTS, planes, lanes), f32),
            pltpu.VMEM((6, planes, rows, wide), f32),
            pltpu.VMEM((9, planes, rows, wide), f32),
            pltpu.VMEM((9, planes // 2, rows, wide), f32),
            pltpu.VMEM((7, planes // 4 * counts[0], rows // 4 * counts[1], wide), f32),
            dma((TURNS, 4)),
            dma((TURNS, 4)),
            dma((6,)),
            dma((6,)),
            dma((6,)),
            dma((6,)),
            dma((2, 2)),
            dma((2, 2)),
            dma((4, counts[0] * counts[1])),
            dma((4, counts[0] * counts[1])),
            dma((4, 2)),
            dma((4, 2)),
            dma((4,)),
        ],
        compiler_params=pltpu.CompilerParams(
            collective_id=0, has_side_effects=True, vmem_limit_bytes=62 * 1024 * 1024
        ),
    )(conc, right_side, order_field, grain_ids)


def solution(mesh):
    counts = tuple(mesh.shape[axis] for axis in AXES)
    return jax.shard_map(
        functools.partial(body, counts),
        mesh=mesh,
        in_specs=(
            P("gx", "gy", "gz"),
            P("gx", "gy", "gz"),
            P(None, "gx", "gy", "gz"),
            P("gx", "gy", "gz", None),
        ),
        out_specs=(P("gx", "gy", "gz"), P("gx", "gy", "gz")),
        check_vma=False,
    )
```
